512 devices in a mesh: seq: 128 (over z, y, core), pack: 4 (over x).
Axes of the slice: x: 4, y: 8, z: 8, core: 2. Of those that a mesh axis runs over, the one named last changes fastest.
Arguments:
- queries: bfloat16 [131072, 2048], P(('pack', 'seq')), parts along dimension 0, may hold values from -10 to 10
- keys: bfloat16 [131072, 512], P(('pack', 'seq')), parts along dimension 0, may hold values from -10 to 10
- values: bfloat16 [131072, 512], P(('pack', 'seq')), parts along dimension 0, may hold values from -6 to 6
- lengths: int32 [512], P('pack'), parts along dimension 0, may hold values from 1 to 4096, 32768 in all
- home: int32 [1024], P('pack'), parts along dimension 0, may hold values from 0 to 127, as said below
Outputs:
- attended: bfloat16 [131072, 2048], P(('pack', 'seq')), parts along dimension 0
The draws below stay inside these ranges and needn't reach their ends.
There are 4 independent parts, one for each index of `pack`. The reference program is written for one: setup_inputs(seed, part) draws one part's arguments, and reference() takes and returns one part's arrays. A program takes and returns all parts, laid end to end along the dimension named above; each array names one. Nothing has to cross between parts.
Inputs may be any that keep to these rules, and one draw needn't show every extreme that they name: Block b covers positions b * 128 to b * 128 + 127. home[b] is 2 * (b // 4) or that plus one, and every device index is home of exactly 2 blocks.
All inputs are finite; a program needn't handle non-finite values.
Results may differ from the reference program's by a relative error of at most 0.0033.
Values may be sent and summed in bfloat16 or wider, within the bound.
No kernel may reach another device: no remote copies, remote signals or barrier semaphores. Data moves between devices by JAX's collectives and lax.ppermute only.
A program may use at most 64 MiB of HBM per device.

```python
import math
import jax
import jax.numpy as jnp
import numpy as np
from jax import lax

QH = 16
KVH = 4
HD = 128
BLOCK = 128
GROUP = 4
WINDOW = 2048
TOKENS = 32768
DOCS = 128
MOST_LEN = 4096
NBLK = 256
BPD = 2


def draw_queries(key, part):
    normal_part = jnp.clip(jax.random.normal(jax.random.fold_in(key, 11), (TOKENS, QH * HD), jnp.float32), -6.0, 6.0)
    return normal_part.astype(jnp.bfloat16)


def draw_keys(key, part):
    normal_part = jnp.clip(jax.random.normal(jax.random.fold_in(key, 12), (TOKENS, KVH * HD), jnp.float32), -6.0, 6.0)
    return normal_part.astype(jnp.bfloat16)


def draw_home(key, part):
    group_count = NBLK // (2 * BPD)
    group_keys = jax.random.split(jax.random.fold_in(key, 21), group_count)
    shuffles = jax.vmap(lambda one_key: jax.random.permutation(one_key, 2 * BPD))(group_keys)
    ranking = jnp.argsort(shuffles, axis=1, stable=True).astype(jnp.int32)
    group_ids = jnp.arange(group_count, dtype=jnp.int32)[:, None]
    home = 2 * group_ids + (ranking >= BPD).astype(jnp.int32)
    return home.reshape(NBLK).astype(jnp.int32)


def block_levels(key, dims, shards, least, top_value):
    def one(axis_at, shards_of):
        heights = jax.random.uniform(jax.random.fold_in(jax.random.fold_in(key, 6), axis_at), (shards_of,), jnp.float32, least / len(shards), top_value / len(shards))
        return jnp.repeat(jnp.exp(heights), dims[axis_at] // shards_of).reshape((-1,) + (1,) * (len(dims) - axis_at - 1))

    level = one(*shards[0])
    for cut in shards[1:]:
        level = level * one(*cut)
    return level


def split_up(amount, total, reach, lean):
    weights = [(1 << 20) // math.isqrt(standing ** lean) + 1 for standing in range(2, amount + 1)]
    rest, counts = total - reach - (amount - 1), [1] * (amount - 1)
    while rest > 0:
        movable = [i for i in range(amount - 1) if counts[i] < reach]
        pool, left = sum([weights[i] for i in movable]), rest
        for i in movable:
            extra = min(reach - counts[i], max(1, left * weights[i] // pool), rest)
            counts[i] = counts[i] + extra
            rest = rest - extra
    return np.array([reach] + counts)


def uneven(stream_key, count, total, bound, skew):
    if count == 2:
        one = jax.random.randint(stream_key, (), max(1, total - bound), min(bound, total - 1) + 1)
        return jnp.stack([one, total - one])
    sizes = jnp.asarray(split_up(count, total, bound, skew), jnp.int32)
    twos = (count - 1) // 2
    giver, taker = sizes[1:1 + 2 * twos:2], sizes[2:2 + 2 * twos:2]
    margin = jnp.minimum(giver - 1, bound - taker)
    moved = jax.random.randint(jax.random.fold_in(stream_key, 1), (twos,), 0, 1 << 20) % (margin + 1)
    sizes = sizes.at[1:1 + 2 * twos:2].set(giver - moved).at[2:2 + 2 * twos:2].set(taker + moved)
    return sizes[jax.random.permutation(jax.random.fold_in(stream_key, 2), count)]


def gaussian(own_key, dims, deviation, reach, shards=(), kind=jnp.bfloat16):
    drawn = jax.random.normal(own_key, dims, jnp.float32) * deviation
    if len(shards) > 0:
        drawn = block_levels(own_key, dims, shards, -0.22, 0.18) * drawn
    return jnp.clip(drawn, min=-reach, max=reach).astype(kind)


def setup_inputs(seed: int = 0, part: int = 0) -> dict:
    arg_keys = jax.random.split(jax.random.key(seed), 6)
    part_keys = jax.random.split(jax.random.fold_in(arg_keys[5], part), 6)
    queries = draw_queries(jax.random.fold_in(jax.random.fold_in(arg_keys[5], part), 71), part)
    keys = draw_keys(jax.random.fold_in(jax.random.fold_in(arg_keys[5], part), 71), part)
    values = gaussian(part_keys[2], (TOKENS, KVH * HD), 1.0, 6.0, ((0, 128),))
    lengths = uneven(part_keys[3], DOCS, TOKENS, MOST_LEN, 2).astype(jnp.int32)
    home = draw_home(jax.random.fold_in(jax.random.fold_in(arg_keys[5], part), 71), part)
    return dict(queries=queries, keys=keys, values=values, lengths=lengths, home=home)


def doc_first_of(lengths, positions):
    doc_ends = jnp.cumsum(lengths).astype(jnp.int32)
    doc_starts = (doc_ends - lengths).astype(jnp.int32)
    chosen = jnp.where(doc_starts[None, :] <= positions[:, None], doc_starts[None, :], 0)
    return jnp.max(chosen, axis=1).astype(jnp.int32)


def reference(queries, keys, values, lengths, home):
    positions = jnp.arange(TOKENS, dtype=jnp.int32)
    doc_first = doc_first_of(lengths, positions)
    zero_rows = jnp.zeros((WINDOW, KVH * HD), jnp.bfloat16)
    keys_padded = jnp.concatenate([zero_rows, keys], axis=0)
    values_padded = jnp.concatenate([zero_rows, values], axis=0)

    def one_block(block_id):
        row_start = (block_id * BLOCK).astype(jnp.int32)
        query_rows = lax.dynamic_slice_in_dim(queries, row_start, BLOCK, 0).astype(jnp.float32).reshape(BLOCK, KVH, GROUP, HD)
        key_rows = lax.dynamic_slice_in_dim(keys_padded, row_start, WINDOW + BLOCK, 0).astype(jnp.float32).reshape(WINDOW + BLOCK, KVH, HD)
        value_rows = lax.dynamic_slice_in_dim(values_padded, row_start, WINDOW + BLOCK, 0).astype(jnp.float32).reshape(WINDOW + BLOCK, KVH, HD)
        query_pos = row_start + jnp.arange(BLOCK, dtype=jnp.int32)
        key_pos = row_start - WINDOW + jnp.arange(WINDOW + BLOCK, dtype=jnp.int32)
        first_rows = lax.dynamic_slice_in_dim(doc_first, row_start, BLOCK, 0)
        allowed = (key_pos[None, :] <= query_pos[:, None]) & (key_pos[None, :] > query_pos[:, None] - WINDOW) & (key_pos[None, :] >= first_rows[:, None])
        scores = jnp.einsum("qhgd,khd->hgqk", query_rows, key_rows) * (HD ** -0.5)
        scores = jnp.where(allowed, scores, jnp.float32(-1e30))
        row_max = jnp.max(scores, axis=-1, keepdims=True)
        weights = jnp.where(allowed, jnp.exp(scores - row_max), jnp.float32(0.0))
        denominator = jnp.sum(weights, axis=-1)
        rounded = lax.optimization_barrier(weights.astype(jnp.bfloat16)).astype(jnp.float32)
        numerator = jnp.einsum("hgqk,khd->hgqd", rounded, value_rows)
        mixed = numerator / denominator[..., None]
        return mixed.transpose(2, 0, 1, 3).reshape(BLOCK, QH * HD).astype(jnp.bfloat16)

    block_outputs = lax.map(one_block, jnp.arange(NBLK, dtype=jnp.int32))
    slot_order = jnp.argsort(home, stable=True).astype(jnp.int32)
    return block_outputs[slot_order].reshape(TOKENS, QH * HD)
```

```python
import functools
import math

import jax
import jax.numpy as jnp
from jax import lax
from jax.experimental import pallas as pl
from jax.experimental.pallas import tpu as pltpu
from jax.sharding import PartitionSpec as P

HD = 128
BLOCK = 128
WINDOW = 2048
ROWS = 256
HEADS = 8
HALF = HEADS * HD
LOG2E = math.log2(math.e)
FACTOR = HD**-0.5 * LOG2E
NEG = -1e30
VLIM = 48 * 1024 * 1024


def vmem(shape, dtype):
    return pltpu.VMEM(shape, dtype)


def params():
    return pltpu.CompilerParams(vmem_limit_bytes=VLIM)


VSPEC = pl.BlockSpec(memory_space=pltpu.VMEM)
SSPEC = pl.BlockSpec(memory_space=pltpu.SMEM)


def pack_kernel(meta, q, k, v, near, cross, swap):
    core = meta[0]
    other = 1 - core
    mine = pl.ds(pl.multiple_of(core * 256, 256), 256)
    theirs = pl.ds(pl.multiple_of(other * 256, 256), 256)
    near[:, 0:256] = k[:, mine]
    near[:, 256:512] = v[:, mine]
    k_other = k[:, theirs]
    v_other = v[:, theirs]
    cross[:, 0:256] = k_other
    cross[:, 256:512] = v_other
    swap[:, 0:HALF] = q[:, pl.ds(pl.multiple_of(other * HALF, HALF), HALF)]
    swap[:, HALF : HALF + 256] = k_other
    swap[:, HALF + 256 : HALF + 512] = v_other


def tile_update(q, kv, k_col, lo, key_pos_base, row_pos, row, acc, top, low, first, masked):
    rows = pl.ds(pl.multiple_of(row, BLOCK), BLOCK)
    if masked:
        key_pos = key_pos_base + lax.broadcasted_iota(jnp.int32, (BLOCK, ROWS), 1)
        last = row_pos + lax.broadcasted_iota(jnp.int32, (BLOCK, ROWS), 0)
        allowed = (key_pos <= last) & (key_pos >= lo[rows, :])
        bias = jnp.where(allowed, jnp.float32(0.0), jnp.float32(NEG))
    for head in range(HEADS):
        cols = pl.ds(head * HD, HD)
        kvh = head // 4
        keys = kv[:, k_col + kvh * HD : k_col + (kvh + 1) * HD]
        vals = kv[:, k_col + 256 + kvh * HD : k_col + 256 + (kvh + 1) * HD]
        s = lax.dot_general(
            q[rows, cols], keys, (((1,), (1,)), ((), ())), preferred_element_type=jnp.float32
        )
        if masked:
            s = s + bias
        peak = jnp.max(jnp.maximum(s[:, :HD], s[:, HD:]), axis=1, keepdims=True)
        if first:
            new_top = jnp.broadcast_to(peak, (BLOCK, HD))
        else:
            old_top = top[rows, cols]
            new_top = jnp.maximum(old_top, peak)
            keep = jnp.exp2((old_top - new_top) * FACTOR)
        shift = new_top * FACTOR
        p0 = jnp.exp2(s[:, :HD] * FACTOR - shift)
        p1 = jnp.exp2(s[:, HD:] * FACTOR - shift)
        p = jnp.concatenate([p0, p1], axis=1).astype(jnp.bfloat16)
        mixed = jnp.dot(p, vals, preferred_element_type=jnp.float32)
        part = p0 + p1
        top[rows, cols] = new_top
        if first:
            low[rows, cols] = part
            acc[rows, cols] = mixed
        else:
            low[rows, cols] = low[rows, cols] * keep + part
            acc[rows, cols] = acc[rows, cols] * keep + mixed


def chunk_update(meta, q, kv, k_col, lo, key_base, acc, top, low, blocks):
    def body(block, carry):
        row = block * BLOCK
        row_pos = meta[1 + block]
        lo_first = meta[5 + block]
        lo_last = meta[9 + block]
        some = (key_base <= row_pos + BLOCK - 1) & (key_base + ROWS - 1 >= lo_first)
        full = (key_base + ROWS - 1 <= row_pos) & (key_base >= lo_last)
        args = (q, kv, k_col, lo, key_base, row_pos, row, acc, top, low, False)

        @pl.when(full)
        def _():
            tile_update(*args, False)

        @pl.when(some & jnp.logical_not(full))
        def _():
            tile_update(*args, True)

        return carry

    lax.fori_loop(blocks[0], blocks[1], body, 0)


def first_kernel(meta, lo, q, near, recv, qcat, acc, top, low):
    core = meta[0]
    qcat[0:ROWS, :] = q[:, pl.ds(pl.multiple_of(core * HALF, HALF), HALF)]
    qcat[ROWS : 2 * ROWS, :] = recv[:, 0:HALF]
    own_base = meta[1]
    far_base = meta[3]
    for kv, col, base, start in ((near, 0, own_base, 0), (recv, HALF, far_base, 2)):

        def body(block, carry, kv=kv, col=col, base=base):
            tile_update(
                qcat, kv, col, lo, base, meta[1 + block], block * BLOCK, acc, top, low, True, True
            )
            return carry

        lax.fori_loop(start, start + 2, body, 0)
    chunk_update(meta, qcat, recv, HALF, lo, far_base, acc, top, low, (0, 2))
    chunk_update(meta, qcat, near, 0, lo, own_base, acc, top, low, (2, 4))


def next_kernel(step, cross, meta, lo, q, kv, acc_in, top_in, low_in, acc, top, low):
    base = meta[3 if cross else 1] - step * 2 * ROWS
    chunk_update(meta, q, kv, 0, lo, base, acc, top, low, (0, 4))


def last_kernel(step, cross, meta, lo, q, kv, acc_in, top_in, low_in, keep, send, acc, top, low):
    next_kernel(step, cross, meta, lo, q, kv, acc_in, top_in, low_in, acc, top, low)

    def body(block, carry):
        rows = pl.ds(pl.multiple_of(block * BLOCK, BLOCK), BLOCK)
        slot = pl.ds(pl.multiple_of(meta[17 + block] * BLOCK, BLOCK), BLOCK)

        def write(ref):
            for head in range(HEADS):
                cols = pl.ds(head * HD, HD)
                total = jnp.sum(low[rows, cols], axis=1, keepdims=True)
                ref[slot, cols] = (acc[rows, cols] / total).astype(jnp.bfloat16)

        @pl.when(meta[13 + block] == 1)
        def _():
            write(keep)

        @pl.when(meta[13 + block] == 0)
        def _():
            write(send)

        return carry

    lax.fori_loop(0, 4, body, 0)


def join_kernel(meta, keep, recv, out):
    core = meta[0]
    mine = pl.ds(pl.multiple_of(core * HALF, HALF), HALF)
    theirs = pl.ds(pl.multiple_of((1 - core) * HALF, HALF), HALF)
    out[:, mine] = keep[...]
    out[:, theirs] = recv[...]


STATE = [vmem((2 * ROWS, HALF), jnp.float32)] * 3


def cost(tiles):
    return pl.CostEstimate(
        flops=tiles * 4 * ROWS * ROWS * HD * HEADS,
        bytes_accessed=1 << 20,
        transcendentals=tiles * ROWS * ROWS * HEADS,
    )


def local(queries, keys, values, lengths, home):
    device = lax.axis_index("seq")
    count = lax.axis_size("seq")
    core = device % 2
    partner = device + 1 - 2 * core
    docs = lengths.shape[0]
    order = jnp.arange(docs, dtype=jnp.int32)
    starts = jnp.sum(jnp.where(order[None, :] < order[:, None], lengths[None, :], 0), axis=1)
    block_pos = jnp.stack(
        [device * ROWS, device * ROWS + BLOCK, partner * ROWS, partner * ROWS + BLOCK]
    ).astype(jnp.int32)
    row_pos = (block_pos[:, None] + jnp.arange(BLOCK, dtype=jnp.int32)[None, :]).reshape(-1)
    doc_first = jnp.max(jnp.where(starts[None, :] <= row_pos[:, None], starts[None, :], 0), axis=1)
    lo = jnp.maximum(doc_first, row_pos - (WINDOW - 1))
    by_block = lo.reshape(4, BLOCK)
    base_block = (device - core) * 2
    group_home = lax.dynamic_slice_in_dim(home, base_block, 4, 0)
    ranks = jnp.sum(
        (group_home[None, :] == group_home[:, None])
        & (jnp.arange(4)[None, :] < jnp.arange(4)[:, None]),
        axis=1,
    ).astype(jnp.int32)
    mine = (group_home == device).astype(jnp.int32)
    turn = jnp.where(core == 0, jnp.arange(4), (jnp.arange(4) + 2) % 4)
    pick = (turn[:, None] == jnp.arange(4)[None, :]).astype(jnp.int32)
    meta = jnp.concatenate(
        [
            core[None].astype(jnp.int32),
            block_pos,
            by_block[:, 0],
            by_block[:, -1],
            jnp.sum(pick * mine[None, :], axis=1),
            jnp.sum(pick * ranks[None, :], axis=1),
        ]
    ).astype(jnp.int32)
    lo = lo[:, None]

    near, cross, swap = pl.pallas_call(
        pack_kernel,
        out_shape=[
            vmem((ROWS, 512), jnp.bfloat16),
            vmem((ROWS, 512), jnp.bfloat16),
            vmem((ROWS, HALF + 512), jnp.bfloat16),
        ],
        in_specs=[SSPEC] + [VSPEC] * 3,
        out_specs=[VSPEC] * 3,
        compiler_params=params(),
        name="pack",
    )(core[None].astype(jnp.int32), queries, keys, values)

    same = [(i, i + 2) for i in range(count - 2)]
    other = [(i, (i ^ 1) + 2) for i in range(count - 2)]
    pair = [(i, i ^ 1) for i in range(count)]
    shift = functools.partial(lax.ppermute, axis_name="seq")
    chunks = [[shift(near, perm=same)], [shift(cross, perm=other)]]
    recv = shift(swap, perm=pair)
    for step in range(1, 4):
        for chain in chunks:
            chain.append(shift(chain[-1], perm=same))

    qcat, *state = pl.pallas_call(
        first_kernel,
        out_shape=[vmem((2 * ROWS, HALF), jnp.bfloat16)] + STATE,
        in_specs=[SSPEC] + [VSPEC] * 4,
        out_specs=[VSPEC] * 4,
        compiler_params=params(),
        cost_estimate=cost(3),
        name="first",
    )(meta, lo, queries, near, recv)
    for step in range(4):
        for side in range(2):
            last = step == 3 and side == 1
            kernel = last_kernel if last else next_kernel
            extra = [vmem((ROWS, HALF), jnp.bfloat16)] * 2 if last else []
            kv = chunks[side][step]
            results = pl.pallas_call(
                functools.partial(kernel, step + 1, side == 1),
                out_shape=extra + STATE,
                in_specs=[SSPEC] + [VSPEC] * 6,
                out_specs=[VSPEC] * (3 + len(extra)),
                input_output_aliases={4: len(extra), 5: len(extra) + 1, 6: len(extra) + 2},
                compiler_params=params(),
                cost_estimate=cost(2),
                name="last" if last else "next",
            )(meta, lo, qcat, kv, *state)
            state = results[len(extra) :]
    keep, send = results[:2]
    got = shift(send, perm=pair)
    return pl.pallas_call(
        join_kernel,
        out_shape=jax.ShapeDtypeStruct((ROWS, 2 * HALF), jnp.bfloat16),
        in_specs=[SSPEC] + [VSPEC] * 2,
        out_specs=VSPEC,
        compiler_params=params(),
        name="join",
    )(core[None].astype(jnp.int32), keep, got)


def solution(mesh):
    placed = (
        P(("pack", "seq"), None),
        P(("pack", "seq"), None),
        P(("pack", "seq"), None),
        P("pack"),
        P("pack"),
    )
    return jax.shard_map(
        local, mesh=mesh, in_specs=placed, out_specs=P(("pack", "seq"), None), check_vma=False
    )
```

```python
import functools
import math

import jax
import jax.numpy as jnp
from jax import lax
from jax.experimental import pallas as pl
from jax.experimental.pallas import tpu as pltpu
from jax.sharding import PartitionSpec as P

HD = 128
BLOCK = 128
WINDOW = 2048
ROWS = 256
HEADS = 8
HALF = HEADS * HD
LOG2E = math.log2(math.e)
FACTOR = HD**-0.5 * LOG2E
NEG = -1e30
COSTS = (5.0, 4.0)
VLIM = 32 * 1024 * 1024


def vmem(shape, dtype):
    return pltpu.VMEM(shape, dtype)


def params():
    return pltpu.CompilerParams(vmem_limit_bytes=VLIM)


VSPEC = pl.BlockSpec(memory_space=pltpu.VMEM)
SSPEC = pl.BlockSpec(memory_space=pltpu.SMEM)


def pack_kernel(meta, q, k, v, near, cross, swap):
    core = meta[0]
    other = 1 - core
    mine = pl.ds(pl.multiple_of(core * 256, 256), 256)
    theirs = pl.ds(pl.multiple_of(other * 256, 256), 256)
    near[:, 0:256] = k[:, mine]
    near[:, 256:512] = v[:, mine]
    k_other = k[:, theirs]
    v_other = v[:, theirs]
    cross[:, 0:256] = k_other
    cross[:, 256:512] = v_other
    swap[:, 0:HALF] = q[:, pl.ds(pl.multiple_of(other * HALF, HALF), HALF)]
    swap[:, HALF : HALF + 256] = k_other
    swap[:, HALF + 256 : HALF + 512] = v_other


def tile_update(q, kv, k_col, lo, key_pos_base, row_pos, row, acc, top, low, first, masked):
    rows = pl.ds(pl.multiple_of(row, BLOCK), BLOCK)
    if masked:
        key_pos = key_pos_base + lax.broadcasted_iota(jnp.int32, (BLOCK, ROWS), 1)
        last = row_pos + lax.broadcasted_iota(jnp.int32, (BLOCK, ROWS), 0)
        allowed = (key_pos <= last) & (key_pos >= lo[rows, :])
        bias = jnp.where(allowed, jnp.float32(0.0), jnp.float32(NEG))
    for head in range(HEADS):
        cols = pl.ds(head * HD, HD)
        kvh = head // 4
        keys = kv[:, k_col + kvh * HD : k_col + (kvh + 1) * HD]
        vals = kv[:, k_col + 256 + kvh * HD : k_col + 256 + (kvh + 1) * HD]
        s = lax.dot_general(
            q[rows, cols], keys, (((1,), (1,)), ((), ())), preferred_element_type=jnp.float32
        )
        if masked:
            s = s + bias
        peak = jnp.max(jnp.maximum(s[:, :HD], s[:, HD:]), axis=1, keepdims=True)
        if first:
            new_top = jnp.broadcast_to(peak, (BLOCK, HD))
        else:
            old_top = top[rows, cols]
            new_top = jnp.maximum(old_top, peak)
            keep = jnp.exp2((old_top - new_top) * FACTOR)
        shift = new_top * FACTOR
        p0 = jnp.exp2(s[:, :HD] * FACTOR - shift)
        p1 = jnp.exp2(s[:, HD:] * FACTOR - shift)
        p = jnp.concatenate([p0, p1], axis=1).astype(jnp.bfloat16)
        mixed = jnp.dot(p, vals, preferred_element_type=jnp.float32)
        part = p0 + p1
        top[rows, cols] = new_top
        if first:
            low[rows, cols] = part
            acc[rows, cols] = mixed
        else:
            low[rows, cols] = low[rows, cols] * keep + part
            acc[rows, cols] = acc[rows, cols] * keep + mixed


def chunk_update(meta, q, kv, k_col, lo, key_base, acc, top, low, blocks):
    def body(block, carry):
        row = block * BLOCK
        row_pos = meta[1 + block]
        lo_first = meta[5 + block]
        lo_last = meta[9 + block]
        some = (key_base <= row_pos + BLOCK - 1) & (key_base + ROWS - 1 >= lo_first)
        full = (key_base + ROWS - 1 <= row_pos) & (key_base >= lo_last)
        args = (q, kv, k_col, lo, key_base, row_pos, row, acc, top, low, False)

        @pl.when(full)
        def _():
            tile_update(*args, False)

        @pl.when(some & jnp.logical_not(full))
        def _():
            tile_update(*args, True)

        return carry

    lax.fori_loop(blocks[0], blocks[1], body, 0)


def first_kernel(meta, lo, q, near, recv, qcat, acc, top, low, token):
    core = meta[0]
    qcat[0:ROWS, :] = q[:, pl.ds(pl.multiple_of(core * HALF, HALF), HALF)]
    qcat[ROWS : 2 * ROWS, :] = recv[:, 0:HALF]
    own_base = meta[1]
    far_base = meta[3]
    for kv, col, base, start in ((near, 0, own_base, 0), (recv, HALF, far_base, 2)):

        def body(block, carry, kv=kv, col=col, base=base):
            tile_update(
                qcat, kv, col, lo, base, meta[1 + block], block * BLOCK, acc, top, low, True, True
            )
            return carry

        lax.fori_loop(start, start + 2, body, 0)
    chunk_update(meta, qcat, recv, HALF, lo, far_base, acc, top, low, (0, 2))
    chunk_update(meta, qcat, near, 0, lo, own_base, acc, top, low, (2, 4))


def next_kernel(step, cross, meta, lo, q, kv, acc_in, top_in, low_in, acc, top, low, *token):
    base = meta[3 if cross else 1] - step * 2 * ROWS
    chunk_update(meta, q, kv, 0, lo, base, acc, top, low, (0, 4))


def last_kernel(step, cross, meta, lo, q, kv, acc_in, top_in, low_in, keep, send, acc, top, low):
    next_kernel(step, cross, meta, lo, q, kv, acc_in, top_in, low_in, acc, top, low)

    def body(block, carry):
        rows = pl.ds(pl.multiple_of(block * BLOCK, BLOCK), BLOCK)
        slot = pl.ds(pl.multiple_of(meta[17 + block] * BLOCK, BLOCK), BLOCK)

        def write(ref):
            for head in range(HEADS):
                cols = pl.ds(head * HD, HD)
                total = jnp.sum(low[rows, cols], axis=1, keepdims=True)
                ref[slot, cols] = (acc[rows, cols] / total).astype(jnp.bfloat16)

        @pl.when(meta[13 + block] == 1)
        def _():
            write(keep)

        @pl.when(meta[13 + block] == 0)
        def _():
            write(send)

        return carry

    lax.fori_loop(0, 4, body, 0)


def join_kernel(meta, keep, recv, out):
    core = meta[0]
    mine = pl.ds(pl.multiple_of(core * HALF, HALF), HALF)
    theirs = pl.ds(pl.multiple_of((1 - core) * HALF, HALF), HALF)
    out[:, mine] = keep[...]
    out[:, theirs] = recv[...]


STATE = [vmem((2 * ROWS, HALF), jnp.float32)] * 3


TOKEN = [vmem((8, 128), jnp.float32)]
ASPEC = pl.BlockSpec(memory_space=pl.ANY)


def touch(buffer, token):
    return pl.pallas_call(
        lambda buffer_ref, token_ref, out_ref: None,
        out_shape=vmem(buffer.shape, buffer.dtype),
        in_specs=[ASPEC, ASPEC],
        out_specs=ASPEC,
        input_output_aliases={0: 0},
        compiler_params=pltpu.CompilerParams(vmem_limit_bytes=1024 * 1024),
        name="touch",
    )(near_core(buffer), near_core(token))


def cost(micros):
    return pl.CostEstimate(
        flops=int(micros * 1.15e9), bytes_accessed=1 << 20, transcendentals=1 << 20
    )


def near_core(x):
    return pltpu.with_memory_space_constraint(x, pltpu.VMEM)


def local(queries, keys, values, lengths, home):
    device = lax.axis_index("seq")
    count = lax.axis_size("seq")
    core = device % 2
    partner = device + 1 - 2 * core
    docs = lengths.shape[0]
    order = jnp.arange(docs, dtype=jnp.int32)
    starts = jnp.sum(jnp.where(order[None, :] < order[:, None], lengths[None, :], 0), axis=1)
    block_pos = jnp.stack(
        [device * ROWS, device * ROWS + BLOCK, partner * ROWS, partner * ROWS + BLOCK]
    ).astype(jnp.int32)
    row_pos = (block_pos[:, None] + jnp.arange(BLOCK, dtype=jnp.int32)[None, :]).reshape(-1)
    doc_first = jnp.max(jnp.where(starts[None, :] <= row_pos[:, None], starts[None, :], 0), axis=1)
    lo = jnp.maximum(doc_first, row_pos - (WINDOW - 1))
    by_block = lo.reshape(4, BLOCK)
    base_block = (device - core) * 2
    group_home = lax.dynamic_slice_in_dim(home, base_block, 4, 0)
    ranks = jnp.sum(
        (group_home[None, :] == group_home[:, None])
        & (jnp.arange(4)[None, :] < jnp.arange(4)[:, None]),
        axis=1,
    ).astype(jnp.int32)
    mine = (group_home == device).astype(jnp.int32)
    turn = jnp.where(core == 0, jnp.arange(4), (jnp.arange(4) + 2) % 4)
    pick = (turn[:, None] == jnp.arange(4)[None, :]).astype(jnp.int32)
    meta = jnp.concatenate(
        [
            core[None].astype(jnp.int32),
            block_pos,
            by_block[:, 0],
            by_block[:, -1],
            jnp.sum(pick * mine[None, :], axis=1),
            jnp.sum(pick * ranks[None, :], axis=1),
        ]
    ).astype(jnp.int32)
    lo = lo[:, None]

    near, cross, swap = pl.pallas_call(
        pack_kernel,
        out_shape=[
            vmem((ROWS, 512), jnp.bfloat16),
            vmem((ROWS, 512), jnp.bfloat16),
            vmem((ROWS, HALF + 512), jnp.bfloat16),
        ],
        in_specs=[SSPEC] + [VSPEC] * 3,
        out_specs=[VSPEC] * 3,
        compiler_params=params(),
        name="pack",
    )(core[None].astype(jnp.int32), queries, keys, values)

    same = [(i, i + 2) for i in range(count - 2)]
    other = [(i, (i ^ 1) + 2) for i in range(count - 2)]
    pair = [(i, i ^ 1) for i in range(count)]
    shift = functools.partial(lax.ppermute, axis_name="seq")
    arrived = [shift(near, perm=same), shift(cross, perm=other)]
    recv = shift(swap, perm=pair)

    qcat, *state = pl.pallas_call(
        first_kernel,
        out_shape=[vmem((2 * ROWS, HALF), jnp.bfloat16)] + STATE + TOKEN,
        in_specs=[SSPEC] + [VSPEC] * 4,
        out_specs=[VSPEC] * 4 + [ASPEC],
        compiler_params=params(),
        cost_estimate=cost(COSTS[0]),
        name="first",
    )(meta, near_core(lo), queries, near_core(near), near_core(recv))
    token = state.pop()
    for index in range(8):
        step, side = index // 2, index % 2
        last = index == 7
        kv = arrived[index]
        if index < 6:
            held = touch(kv, token)
            arrived.append(shift(held, perm=same))
            kv = held
        kernel = last_kernel if last else next_kernel
        extra = [vmem((ROWS, HALF), jnp.bfloat16)] * 2 if last else []
        results = pl.pallas_call(
            functools.partial(kernel, step + 1, side == 1),
            out_shape=extra + STATE + ([] if last else TOKEN),
            in_specs=[SSPEC] + [VSPEC] * 6,
            out_specs=[VSPEC] * (3 + len(extra)) + ([] if last else [ASPEC]),
            input_output_aliases={4: len(extra), 5: len(extra) + 1, 6: len(extra) + 2},
            compiler_params=params(),
            cost_estimate=cost(COSTS[1]),
            name="last" if last else "next",
        )(meta, near_core(lo), near_core(qcat), near_core(kv), *[near_core(x) for x in state])
        state = results[len(extra) : len(extra) + 3]
        token = results[-1]
    keep, send = results[:2]
    got = shift(send, perm=pair)
    return pl.pallas_call(
        join_kernel,
        out_shape=jax.ShapeDtypeStruct((ROWS, 2 * HALF), jnp.bfloat16),
        in_specs=[SSPEC] + [VSPEC] * 2,
        out_specs=VSPEC,
        compiler_params=params(),
        name="join",
    )(core[None].astype(jnp.int32), near_core(keep), near_core(got))


def solution(mesh):
    placed = (
        P(("pack", "seq"), None),
        P(("pack", "seq"), None),
        P(("pack", "seq"), None),
        P("pack"),
        P("pack"),
    )
    return jax.shard_map(
        local, mesh=mesh, in_specs=placed, out_specs=P(("pack", "seq"), None), check_vma=False
    )
```

```python
import functools
import math

import jax
import jax.numpy as jnp
from jax import lax
from jax.experimental import pallas as pl
from jax.experimental.pallas import tpu as pltpu
from jax.sharding import PartitionSpec as P

HD = 128
BLOCK = 128
WINDOW = 2048
ROWS = 256
HEADS = 8
GROUP = 4
HALF = HEADS * HD
KVW = 512
FACTOR = HD**-0.5 * math.log2(math.e)
NEG = -1e30
PLAN = 20.0
VLIM = 24 * 1024 * 1024
VSPEC = pl.BlockSpec(memory_space=pltpu.VMEM)
SSPEC = pl.BlockSpec(memory_space=pltpu.SMEM)
ASPEC = pl.BlockSpec(memory_space=pl.ANY)
STATE = [pltpu.VMEM((2 * ROWS, HALF), jnp.float32)] * 3
TOKEN = [pltpu.VMEM((8, 128), jnp.float32)]
POS, LOW_FIRST, LOW_LAST, MINE, SLOT = 1, 5, 9, 13, 17


def params(limit=VLIM):
    return pltpu.CompilerParams(vmem_limit_bytes=limit)


def cost(micros):
    return pl.CostEstimate(
        flops=int(micros * 1.15e9), bytes_accessed=1 << 20, transcendentals=1 << 20
    )


def fast(x):
    return pltpu.with_memory_space_constraint(x, pltpu.VMEM)


def touch(buffer, token):
    return pl.pallas_call(
        lambda buffer_ref, token_ref, out_ref: None,
        out_shape=pltpu.VMEM(buffer.shape, buffer.dtype),
        in_specs=[ASPEC, ASPEC],
        out_specs=ASPEC,
        input_output_aliases={0: 0},
        compiler_params=params(1024 * 1024),
        name="touch",
    )(fast(buffer), fast(token))


def near_kernel(k, v, near, sems):
    core = lax.rem(lax.axis_index("seq"), 2)
    cols = pl.ds(pl.multiple_of(core * 256, 256), 256)
    copies = [
        pltpu.make_async_copy(source.at[:, cols], near.at[:, i * 256 : i * 256 + 256], sems.at[i])
        for i, source in enumerate((k, v))
    ]
    for copy in copies:
        copy.start()
    for copy in copies:
        copy.wait()


def pack_kernel(q, k, v, near, cross, swap, own, sems):
    core = lax.rem(lax.axis_index("seq"), 2)
    other = 1 - core

    def cols(index, width):
        return pl.ds(pl.multiple_of(index * width, width), width)

    moves = [
        (k.at[:, cols(other, 256)], cross.at[:, 0:256]),
        (v.at[:, cols(other, 256)], cross.at[:, 256:512]),
        (q.at[:, cols(other, HALF)], swap.at[:, 0:HALF]),
        (k.at[:, cols(other, 256)], swap.at[:, HALF : HALF + 256]),
        (v.at[:, cols(other, 256)], swap.at[:, HALF + 256 : HALF + 512]),
        (q.at[:, cols(core, HALF)], own),
    ]
    copies = [
        pltpu.make_async_copy(source, target, sems.at[i])
        for i, (source, target) in enumerate(moves)
    ]
    for copy in copies:
        copy.start()
    for copy in copies:
        copy.wait()


def plan_kernel(lengths, home, meta, low_key):
    device = lax.axis_index("seq")
    core = lax.rem(device, 2)
    docs = lengths.shape[1]
    wide = jnp.broadcast_to(lengths[...].astype(jnp.float32), (docs, docs))
    before = lax.broadcasted_iota(jnp.int32, (docs, docs), 0) < lax.broadcasted_iota(
        jnp.int32, (docs, docs), 1
    )
    starts = jnp.sum(jnp.where(before, wide.T, jnp.float32(0.0)), axis=0, keepdims=True)
    meta[0] = core
    for block in range(4):
        half = device if block < 2 else device + 1 - 2 * core
        pos = half * ROWS + (block % 2) * BLOCK
        meta[POS + block] = pos
        for slot, shift in ((LOW_FIRST, 0), (LOW_LAST, BLOCK - 1)):
            at = (pos + shift).astype(jnp.float32)
            first = jnp.max(jnp.where(starts <= at, starts, jnp.float32(0.0)))
            meta[slot + block] = jnp.maximum(
                first.astype(jnp.int32), pos + shift - (WINDOW - 1)
            )
        rows = (pos + lax.broadcasted_iota(jnp.int32, (BLOCK, docs), 0)).astype(jnp.float32)
        first = jnp.max(
            jnp.where(starts <= rows, starts, jnp.float32(0.0)), axis=1, keepdims=True
        )
        low_key[pl.ds(block * BLOCK, BLOCK), :] = jnp.maximum(
            jnp.broadcast_to(first, (BLOCK, docs)), rows - (WINDOW - 1)
        ).astype(jnp.int32)
    homes = [home[(device - core) * 2 + t] for t in range(4)]
    for t in range(4):
        rank = jnp.int32(0)
        for u in range(t):
            rank = rank + (homes[u] == homes[t]).astype(jnp.int32)
        place = lax.rem(t + 2 * core, 4)
        meta[MINE + place] = (homes[t] == device).astype(jnp.int32)
        meta[SLOT + place] = rank


def stacked(ref, rows, kvh):
    return jnp.concatenate(
        [ref[rows, pl.ds((kvh * GROUP + g) * HD, HD)] for g in range(GROUP)], axis=0
    )


def fold(q, q_row, kv, col, state, row, bias=None, first=False, span=ROWS):
    acc, top, low = state
    rows = pl.ds(row, BLOCK)
    for kvh in range(HEADS // GROUP):
        keys = kv[0:span, col + kvh * HD : col + (kvh + 1) * HD]
        vals = kv[0:span, col + 256 + kvh * HD : col + 256 + (kvh + 1) * HD]
        scores = (
            lax.dot_general(
                stacked(q, pl.ds(q_row, BLOCK), kvh),
                keys,
                (((1,), (1,)), ((), ())),
                preferred_element_type=jnp.float32,
            )
            * FACTOR
        )
        if bias is not None:
            scores = scores + jnp.concatenate([bias] * GROUP, axis=0)
        peak = jnp.max(scores, axis=1, keepdims=True)
        if first:
            new = jnp.broadcast_to(peak, (GROUP * BLOCK, HD))
        else:
            old = stacked(top, rows, kvh)
            new = jnp.maximum(old, peak)
            keep = jnp.exp2(old - new)
        weights = jnp.exp2(scores - jnp.concatenate([new] * (span // HD), axis=1))
        mixed = jnp.dot(weights.astype(jnp.bfloat16), vals, preferred_element_type=jnp.float32)
        part = weights[:, :HD]
        if span > HD:
            part = part + weights[:, HD:]
        for g in range(GROUP):
            cols = pl.ds((kvh * GROUP + g) * HD, HD)
            cut = slice(g * BLOCK, (g + 1) * BLOCK)
            top[rows, cols] = new[cut]
            if first:
                low[rows, cols] = part[cut]
                acc[rows, cols] = mixed[cut]
            else:
                low[rows, cols] = low[rows, cols] * keep[cut] + part[cut]
                acc[rows, cols] = acc[rows, cols] * keep[cut] + mixed[cut]


def bias_of(meta, low_key, block, key_base, span=ROWS):
    last = meta[POS + block] + lax.broadcasted_iota(jnp.int32, (BLOCK, HD), 0)
    least = low_key[pl.ds(block * BLOCK, BLOCK), :]
    parts = []
    for start in range(0, span, HD):
        key = key_base + start + lax.broadcasted_iota(jnp.int32, (BLOCK, HD), 1)
        allowed = (key <= last) & (key >= least)
        parts.append(jnp.where(allowed, jnp.float32(0.0), jnp.float32(NEG)))
    return jnp.concatenate(parts, axis=1)


def chunk_update(meta, low_key, halves, kv, col, key_base, state):
    some, full = [], []
    for _, block in halves:
        some.append(
            (key_base <= meta[POS + block + 1] + BLOCK - 1)
            & (key_base + ROWS - 1 >= meta[LOW_FIRST + block])
        )
        full.append(
            (key_base + ROWS - 1 <= meta[POS + block]) & (key_base >= meta[LOW_LAST + block + 1])
        )
    together = len(halves) == 2
    every = full[0] & full[1] if together else None
    if together:

        @pl.when(every)
        def _():
            for q, block in halves:
                for step in range(2):
                    fold(q, step * BLOCK, kv, col, state, (block + step) * BLOCK)

    for (q, block), any_of, all_of in zip(halves, some, full):
        rest = jnp.logical_not(every) if together else True

        @pl.when(all_of & rest)
        def _(q=q, block=block):
            for step in range(2):
                fold(q, step * BLOCK, kv, col, state, (block + step) * BLOCK)

        @pl.when(any_of & jnp.logical_not(all_of))
        def _(q=q, block=block):
            for step in range(2):
                bias = bias_of(meta, low_key, block + step, key_base)
                fold(q, step * BLOCK, kv, col, state, (block + step) * BLOCK, bias)


def first_kernel(meta, low_key, own, near, recv, acc, top, low, token):
    state = (acc, top, low)
    for q, kv, col, block in ((own, near, 0, 0), (recv, recv, HALF, 2)):
        base = meta[POS + block]
        for step in range(2):
            span = (step + 1) * BLOCK
            bias = bias_of(meta, low_key, block + step, base, span)
            fold(q, step * BLOCK, kv, col, state, (block + step) * BLOCK, bias, True, span)

    @pl.when(meta[0] == 1)
    def _():
        chunk_update(meta, low_key, [(own, 0)], recv, HALF, meta[POS + 2], state)

    @pl.when(meta[0] == 0)
    def _():
        chunk_update(meta, low_key, [(recv, 2)], near, 0, meta[POS], state)


def next_kernel(back, side, meta, low_key, own, recv, kv, *refs):
    acc, top, low = refs[3:6]
    base = meta[POS + side * 2] - back * 2 * ROWS
    chunk_update(meta, low_key, [(own, 0), (recv, 2)], kv, 0, base, (acc, top, low))


def last_kernel(back, side, meta, low_key, own, recv, kv, a, t, d, keep, send, acc, top, low):
    next_kernel(back, side, meta, low_key, own, recv, kv, a, t, d, acc, top, low)
    for block in range(4):
        rows = pl.ds(block * BLOCK, BLOCK)
        slot = pl.ds(pl.multiple_of(meta[SLOT + block] * BLOCK, BLOCK), BLOCK)

        def write(ref, rows=rows, slot=slot):
            for head in range(HEADS):
                cols = pl.ds(head * HD, HD)
                total = jnp.sum(low[rows, cols], axis=1, keepdims=True)
                ref[slot, cols] = (acc[rows, cols] / total).astype(jnp.bfloat16)

        @pl.when(meta[MINE + block] == 1)
        def _(write=write):
            write(keep)

        @pl.when(meta[MINE + block] == 0)
        def _(write=write):
            write(send)


def join_kernel(keep, got, out, sems):
    core = lax.rem(lax.axis_index("seq"), 2)
    copies = []
    for i, (source, half) in enumerate(((keep, core), (got, 1 - core))):
        cols = pl.ds(pl.multiple_of(half * HALF, HALF), HALF)
        copies.append(pltpu.make_async_copy(source, out.at[:, cols], sems.at[i]))
    for copy in copies:
        copy.start()
    for copy in copies:
        copy.wait()


def local(queries, keys, values, lengths, home):
    count = lax.axis_size("seq")
    bf16 = jnp.bfloat16
    hbm = pl.BlockSpec(memory_space=pltpu.HBM)
    near = pl.pallas_call(
        near_kernel,
        out_shape=pltpu.VMEM((ROWS, KVW), bf16),
        in_specs=[hbm] * 2,
        out_specs=VSPEC,
        scratch_shapes=[pltpu.SemaphoreType.DMA((2,))],
        compiler_params=params(60 * 1024 * 1024),
        name="near",
    )(keys, values)
    cross, swap, own = pl.pallas_call(
        pack_kernel,
        out_shape=[
            pltpu.VMEM((ROWS, KVW), bf16),
            pltpu.VMEM((ROWS, HALF + KVW), bf16),
            pltpu.VMEM((ROWS, HALF), bf16),
        ],
        in_specs=[hbm] * 3 + [ASPEC],
        out_specs=[VSPEC] * 3,
        scratch_shapes=[pltpu.SemaphoreType.DMA((6,))],
        compiler_params=params(60 * 1024 * 1024),
        name="pack",
    )(queries, keys, values, fast(near))

    same = [(i, i + 2) for i in range(count - 2)]
    other = [(i, (i ^ 1) + 2) for i in range(count - 2)]
    pair = [(i, i ^ 1) for i in range(count)]
    shift = functools.partial(lax.ppermute, axis_name="seq")
    arrived = [shift(near, perm=same), shift(cross, perm=other)]
    recv = fast(shift(swap, perm=pair))

    meta, low_key = pl.pallas_call(
        plan_kernel,
        out_shape=[pltpu.SMEM((32,), jnp.int32), pltpu.VMEM((2 * ROWS, HD), jnp.int32)],
        in_specs=[VSPEC, SSPEC],
        out_specs=[SSPEC, VSPEC],
        compiler_params=params(),
        cost_estimate=cost(PLAN),
        name="plan",
    )(lengths[None, :], home)
    meta = pltpu.with_memory_space_constraint(meta, pltpu.SMEM)
    low_key, own = fast(low_key), fast(own)

    *state, token = pl.pallas_call(
        first_kernel,
        out_shape=STATE + TOKEN,
        in_specs=[SSPEC] + [VSPEC] * 4,
        out_specs=[VSPEC] * 3 + [ASPEC],
        compiler_params=params(),
        cost_estimate=cost(3.0),
        name="first",
    )(meta, low_key, own, fast(near), recv)
    tokens = [None, token]
    for index in range(6):
        kv = arrived[index]
        if index:
            kv = arrived[index] = touch(kv, tokens[index])
        arrived.append(shift(kv, perm=same))
        if index == 0:
            continue
        state, token = step(index - 1, arrived, meta, low_key, own, recv, state)
        tokens.append(token)
    for index in (5, 6):
        state, token = step(index, arrived, meta, low_key, own, recv, state)
    keep, send = step(7, arrived, meta, low_key, own, recv, state)
    got = shift(send, perm=pair)
    return pl.pallas_call(
        join_kernel,
        out_shape=jax.ShapeDtypeStruct((ROWS, 2 * HALF), bf16),
        in_specs=[VSPEC] * 2,
        out_specs=pl.BlockSpec(memory_space=pltpu.HBM),
        scratch_shapes=[pltpu.SemaphoreType.DMA((2,))],
        compiler_params=params(),
        name="join",
    )(fast(keep), fast(got))


def step(index, arrived, meta, low_key, own, recv, state):
    last = index == 7
    kernel = last_kernel if last else next_kernel
    extra = [pltpu.VMEM((ROWS, HALF), jnp.bfloat16)] * 2 if last else []
    results = pl.pallas_call(
        functools.partial(kernel, index // 2 + 1, index % 2),
        out_shape=extra + STATE + ([] if last else TOKEN),
        in_specs=[SSPEC] + [VSPEC] * 7,
        out_specs=[VSPEC] * (len(extra) + 3) + ([] if last else [ASPEC]),
        input_output_aliases={5 + i: len(extra) + i for i in range(3)},
        compiler_params=params(),
        cost_estimate=cost(2.5),
        name="last" if last else "next",
    )(meta, low_key, own, recv, fast(arrived[index]), *[fast(x) for x in state])
    return results[:2] if last else (results[:3], results[3])


def solution(mesh):
    placed = (
        P(("pack", "seq"), None),
        P(("pack", "seq"), None),
        P(("pack", "seq"), None),
        P("pack"),
        P("pack"),
    )
    return jax.shard_map(
        local, mesh=mesh, in_specs=placed, out_specs=P(("pack", "seq"), None), check_vma=False
    )
```

```python
import functools
import math

import jax
import jax.numpy as jnp
from jax import lax
from jax.experimental import pallas as pl
from jax.experimental.pallas import tpu as pltpu
from jax.sharding import PartitionSpec as P

HD = 128
BLOCK = 128
WINDOW = 2048
ROWS = 256
HEADS = 8
GROUP = 4
HALF = HEADS * HD
KVW = 512
FACTOR = HD**-0.5 * math.log2(math.e)
NEG = -1e30
PLAN = 20.0
VLIM = 24 * 1024 * 1024
VSPEC = pl.BlockSpec(memory_space=pltpu.VMEM)
SSPEC = pl.BlockSpec(memory_space=pltpu.SMEM)
ASPEC = pl.BlockSpec(memory_space=pl.ANY)
STATE = [pltpu.VMEM((2 * ROWS, HALF), jnp.float32)] * 3
TOKEN = [pltpu.VMEM((8, 128), jnp.float32)]
POS, LOW_FIRST, LOW_LAST, MINE, SLOT = 1, 5, 9, 13, 17


def params(limit=VLIM):
    return pltpu.CompilerParams(vmem_limit_bytes=limit)


def cost(micros):
    return pl.CostEstimate(
        flops=int(micros * 1.15e9), bytes_accessed=1 << 20, transcendentals=1 << 20
    )


def fast(x):
    return pltpu.with_memory_space_constraint(x, pltpu.VMEM)


def touch(buffer, token):
    return pl.pallas_call(
        lambda buffer_ref, token_ref, out_ref: None,
        out_shape=pltpu.VMEM(buffer.shape, buffer.dtype),
        in_specs=[ASPEC, ASPEC],
        out_specs=ASPEC,
        input_output_aliases={0: 0},
        compiler_params=params(1024 * 1024),
        name="touch",
    )(fast(buffer), fast(token))


def near_kernel(k, v, near, sems):
    core = lax.rem(lax.axis_index("seq"), 2)
    cols = pl.ds(pl.multiple_of(core * 256, 256), 256)
    copies = [
        pltpu.make_async_copy(source.at[:, cols], near.at[:, i * 256 : i * 256 + 256], sems.at[i])
        for i, source in enumerate((k, v))
    ]
    for copy in copies:
        copy.start()
    for copy in copies:
        copy.wait()


def pack_kernel(q, k, v, near, cross, swap, own, sems):
    core = lax.rem(lax.axis_index("seq"), 2)
    other = 1 - core

    def cols(index, width):
        return pl.ds(pl.multiple_of(index * width, width), width)

    moves = [
        (k.at[:, cols(other, 256)], cross.at[:, 0:256]),
        (v.at[:, cols(other, 256)], cross.at[:, 256:512]),
        (q.at[:, cols(other, HALF)], swap.at[:, 0:HALF]),
        (k.at[:, cols(other, 256)], swap.at[:, HALF : HALF + 256]),
        (v.at[:, cols(other, 256)], swap.at[:, HALF + 256 : HALF + 512]),
        (q.at[:, cols(core, HALF)], own),
    ]
    copies = [
        pltpu.make_async_copy(source, target, sems.at[i])
        for i, (source, target) in enumerate(moves)
    ]
    for copy in copies:
        copy.start()
    for copy in copies:
        copy.wait()


def plan_kernel(lengths, home, meta, low_key):
    device = lax.axis_index("seq")
    core = lax.rem(device, 2)
    docs = lengths.shape[1]
    wide = jnp.broadcast_to(lengths[...].astype(jnp.float32), (docs, docs))
    before = lax.broadcasted_iota(jnp.int32, (docs, docs), 0) < lax.broadcasted_iota(
        jnp.int32, (docs, docs), 1
    )
    starts = jnp.sum(jnp.where(before, wide.T, jnp.float32(0.0)), axis=0, keepdims=True)
    meta[0] = core
    for block in range(4):
        half = device if block < 2 else device + 1 - 2 * core
        pos = half * ROWS + (block % 2) * BLOCK
        meta[POS + block] = pos
        for slot, shift in ((LOW_FIRST, 0), (LOW_LAST, BLOCK - 1)):
            at = (pos + shift).astype(jnp.float32)
            first = jnp.max(jnp.where(starts <= at, starts, jnp.float32(0.0)))
            meta[slot + block] = jnp.maximum(
                first.astype(jnp.int32), pos + shift - (WINDOW - 1)
            )
        rows = (pos + lax.broadcasted_iota(jnp.int32, (BLOCK, docs), 0)).astype(jnp.float32)
        first = jnp.max(
            jnp.where(starts <= rows, starts, jnp.float32(0.0)), axis=1, keepdims=True
        )
        low_key[pl.ds(block * BLOCK, BLOCK), :] = jnp.maximum(
            jnp.broadcast_to(first, (BLOCK, docs)), rows - (WINDOW - 1)
        ).astype(jnp.int32)
    homes = [home[(device - core) * 2 + t] for t in range(4)]
    for t in range(4):
        rank = jnp.int32(0)
        for u in range(t):
            rank = rank + (homes[u] == homes[t]).astype(jnp.int32)
        place = lax.rem(t + 2 * core, 4)
        meta[MINE + place] = (homes[t] == device).astype(jnp.int32)
        meta[SLOT + place] = rank


def row_span(row):
    return pl.ds(row if isinstance(row, int) else pl.multiple_of(row, BLOCK), BLOCK)


def stacked(ref, rows, kvh):
    return jnp.concatenate(
        [ref[rows, pl.ds((kvh * GROUP + g) * HD, HD)] for g in range(GROUP)], axis=0
    )


def fold(q, kv, kv_row, state, row, bias=None, first=False, span=ROWS):
    acc, top, low = state
    rows = row_span(row)
    key_rows = pl.ds(kv_row, span)
    for kvh in range(HEADS // GROUP):
        keys = kv[key_rows, kvh * HD : (kvh + 1) * HD]
        vals = kv[key_rows, 256 + kvh * HD : 256 + (kvh + 1) * HD]
        scores = (
            lax.dot_general(
                stacked(q, rows, kvh),
                keys,
                (((1,), (1,)), ((), ())),
                preferred_element_type=jnp.float32,
            )
            * FACTOR
        )
        if bias is not None:
            scores = scores + jnp.concatenate([bias] * GROUP, axis=0)
        peak = jnp.max(scores, axis=1, keepdims=True)
        if first:
            new = jnp.broadcast_to(peak, (GROUP * BLOCK, HD))
        else:
            old = stacked(top, rows, kvh)
            new = jnp.maximum(old, peak)
            keep = jnp.exp2(old - new)
        weights = jnp.exp2(scores - jnp.concatenate([new] * (span // HD), axis=1))
        mixed = jnp.dot(weights.astype(jnp.bfloat16), vals, preferred_element_type=jnp.float32)
        part = weights[:, :HD]
        if span > HD:
            part = part + weights[:, HD:]
        for g in range(GROUP):
            cols = pl.ds((kvh * GROUP + g) * HD, HD)
            cut = slice(g * BLOCK, (g + 1) * BLOCK)
            top[rows, cols] = new[cut]
            if first:
                low[rows, cols] = part[cut]
                acc[rows, cols] = mixed[cut]
            else:
                low[rows, cols] = low[rows, cols] * keep[cut] + part[cut]
                acc[rows, cols] = acc[rows, cols] * keep[cut] + mixed[cut]


def bias_of(meta, low_key, block, key_base, span=ROWS):
    last = meta[POS + block] + lax.broadcasted_iota(jnp.int32, (BLOCK, HD), 0)
    least = low_key[row_span(block * BLOCK), :]
    parts = []
    for start in range(0, span, HD):
        key = key_base + start + lax.broadcasted_iota(jnp.int32, (BLOCK, HD), 1)
        allowed = (key <= last) & (key >= least)
        parts.append(jnp.where(allowed, jnp.float32(0.0), jnp.float32(NEG)))
    return jnp.concatenate(parts, axis=1)


def half_update(meta, low_key, q, kv, kv_row, half, key_base, state):
    block = half * 2
    last_key = key_base + ROWS - 1
    some = (key_base <= meta[POS + block + 1] + BLOCK - 1) & (last_key >= meta[LOW_FIRST + block])
    full = (last_key <= meta[POS + block]) & (key_base >= meta[LOW_LAST + block + 1])

    @pl.when(full)
    def _():
        for step in range(2):
            fold(q, kv, kv_row, state, (block + step) * BLOCK)

    @pl.when(some & jnp.logical_not(full))
    def _():
        for step in range(2):
            bias = bias_of(meta, low_key, block + step, key_base)
            fold(q, kv, kv_row, state, (block + step) * BLOCK, bias)


def first_kernel(meta, low_key, own, near, recv, q, acc, top, low, token, kv):
    state = (acc, top, low)
    q[0:ROWS, :] = own[...]
    q[ROWS : 2 * ROWS, :] = recv[:, 0:HALF]
    kv[0:ROWS, :] = near[...]
    kv[ROWS : 2 * ROWS, :] = recv[:, HALF : HALF + KVW]

    def body(half, carry):
        kv_row = pl.multiple_of(half * ROWS, ROWS)
        base = meta[POS + half * 2]
        for step in range(2):
            span = (step + 1) * BLOCK
            block = half * 2 + step
            bias = bias_of(meta, low_key, block, base, span)
            fold(q, kv, kv_row, state, block * BLOCK, bias, True, span)
        return carry

    lax.fori_loop(0, 2, body, 0)
    late = 1 - meta[0]
    early_row = pl.multiple_of((1 - late) * ROWS, ROWS)
    half_update(meta, low_key, q, kv, early_row, late, meta[POS + 2 - late * 2], state)


def next_kernel(back, side, meta, low_key, q, kv, *refs):
    state = refs[3:6]
    base = meta[POS + side * 2] - back * 2 * ROWS

    def body(half, carry):
        half_update(meta, low_key, q, kv, 0, half, base, state)
        return carry

    lax.fori_loop(0, 2, body, 0)


def last_kernel(back, side, meta, low_key, q, kv, a, t, d, keep, send, acc, top, low):
    next_kernel(back, side, meta, low_key, q, kv, a, t, d, acc, top, low)

    def body(block, carry):
        rows = row_span(block * BLOCK)
        slot = pl.ds(pl.multiple_of(meta[SLOT + block] * BLOCK, BLOCK), BLOCK)

        def write(ref, rows=rows, slot=slot):
            for head in range(HEADS):
                cols = pl.ds(head * HD, HD)
                total = jnp.sum(low[rows, cols], axis=1, keepdims=True)
                ref[slot, cols] = (acc[rows, cols] / total).astype(jnp.bfloat16)

        @pl.when(meta[MINE + block] == 1)
        def _(write=write):
            write(keep)

        @pl.when(meta[MINE + block] == 0)
        def _(write=write):
            write(send)

        return carry

    lax.fori_loop(0, 4, body, 0)


def join_kernel(keep, got, out, sems):
    core = lax.rem(lax.axis_index("seq"), 2)
    copies = []
    for i, (source, half) in enumerate(((keep, core), (got, 1 - core))):
        cols = pl.ds(pl.multiple_of(half * HALF, HALF), HALF)
        copies.append(pltpu.make_async_copy(source, out.at[:, cols], sems.at[i]))
    for copy in copies:
        copy.start()
    for copy in copies:
        copy.wait()


def local(queries, keys, values, lengths, home):
    count = lax.axis_size("seq")
    bf16 = jnp.bfloat16
    hbm = pl.BlockSpec(memory_space=pltpu.HBM)
    near = pl.pallas_call(
        near_kernel,
        out_shape=pltpu.VMEM((ROWS, KVW), bf16),
        in_specs=[hbm] * 2,
        out_specs=VSPEC,
        scratch_shapes=[pltpu.SemaphoreType.DMA((2,))],
        compiler_params=params(60 * 1024 * 1024),
        name="near",
    )(keys, values)
    cross, swap, own = pl.pallas_call(
        pack_kernel,
        out_shape=[
            pltpu.VMEM((ROWS, KVW), bf16),
            pltpu.VMEM((ROWS, HALF + KVW), bf16),
            pltpu.VMEM((ROWS, HALF), bf16),
        ],
        in_specs=[hbm] * 3 + [ASPEC],
        out_specs=[VSPEC] * 3,
        scratch_shapes=[pltpu.SemaphoreType.DMA((6,))],
        compiler_params=params(60 * 1024 * 1024),
        name="pack",
    )(queries, keys, values, fast(near))

    same = [(i, i + 2) for i in range(count - 2)]
    other = [(i, (i ^ 1) + 2) for i in range(count - 2)]
    pair = [(i, i ^ 1) for i in range(count)]
    shift = functools.partial(lax.ppermute, axis_name="seq")
    arrived = [shift(near, perm=same), shift(cross, perm=other)]
    recv = fast(shift(swap, perm=pair))

    meta, low_key = pl.pallas_call(
        plan_kernel,
        out_shape=[pltpu.SMEM((32,), jnp.int32), pltpu.VMEM((2 * ROWS, HD), jnp.int32)],
        in_specs=[VSPEC, SSPEC],
        out_specs=[SSPEC, VSPEC],
        compiler_params=params(),
        cost_estimate=cost(PLAN),
        name="plan",
    )(lengths[None, :], home)
    meta = pltpu.with_memory_space_constraint(meta, pltpu.SMEM)
    low_key, own = fast(low_key), fast(own)

    q, *state, token = pl.pallas_call(
        first_kernel,
        out_shape=[pltpu.VMEM((2 * ROWS, HALF), bf16)] + STATE + TOKEN,
        in_specs=[SSPEC] + [VSPEC] * 4,
        out_specs=[VSPEC] * 4 + [ASPEC],
        scratch_shapes=[pltpu.VMEM((2 * ROWS, KVW), bf16)],
        compiler_params=params(),
        cost_estimate=cost(3.0),
        name="first",
    )(meta, low_key, own, fast(near), recv)
    tokens = [None, token]
    for index in range(6):
        kv = arrived[index]
        if index:
            kv = arrived[index] = touch(kv, tokens[index])
        arrived.append(shift(kv, perm=same))
        if index == 0:
            continue
        state, token = step(index - 1, arrived, meta, low_key, q, state)
        tokens.append(token)
    for index in (5, 6):
        state, token = step(index, arrived, meta, low_key, q, state)
    keep, send = step(7, arrived, meta, low_key, q, state)
    got = shift(send, perm=pair)
    return pl.pallas_call(
        join_kernel,
        out_shape=jax.ShapeDtypeStruct((ROWS, 2 * HALF), bf16),
        in_specs=[VSPEC] * 2,
        out_specs=pl.BlockSpec(memory_space=pltpu.HBM),
        scratch_shapes=[pltpu.SemaphoreType.DMA((2,))],
        compiler_params=params(),
        name="join",
    )(fast(keep), fast(got))


def step(index, arrived, meta, low_key, q, state):
    last = index == 7
    kernel = last_kernel if last else next_kernel
    extra = [pltpu.VMEM((ROWS, HALF), jnp.bfloat16)] * 2 if last else []
    results = pl.pallas_call(
        functools.partial(kernel, index // 2 + 1, index % 2),
        out_shape=extra + STATE + ([] if last else TOKEN),
        in_specs=[SSPEC] + [VSPEC] * 6,
        out_specs=[VSPEC] * (len(extra) + 3) + ([] if last else [ASPEC]),
        input_output_aliases={4 + i: len(extra) + i for i in range(3)},
        compiler_params=params(),
        cost_estimate=cost(2.5),
        name="last" if last else "next",
    )(meta, low_key, fast(q), fast(arrived[index]), *[fast(x) for x in state])
    return results[:2] if last else (results[:3], results[3])


def solution(mesh):
    placed = (
        P(("pack", "seq"), None),
        P(("pack", "seq"), None),
        P(("pack", "seq"), None),
        P("pack"),
        P("pack"),
    )
    return jax.shard_map(
        local, mesh=mesh, in_specs=placed, out_specs=P(("pack", "seq"), None), check_vma=False
    )
```

```python
import functools
import math

import jax
import jax.numpy as jnp
from jax import lax
from jax.experimental import pallas as pl
from jax.experimental.pallas import tpu as pltpu
from jax.sharding import PartitionSpec as P

HD = 128
BLOCK = 128
WINDOW = 2048
ROWS = 256
HEADS = 8
GROUP = 4
HALF = HEADS * HD
KVW = 512
FACTOR = HD**-0.5 * math.log2(math.e)
NEG = -1e30
PLAN = 20.0
VLIM = 24 * 1024 * 1024
VSPEC = pl.BlockSpec(memory_space=pltpu.VMEM)
SSPEC = pl.BlockSpec(memory_space=pltpu.SMEM)
ASPEC = pl.BlockSpec(memory_space=pl.ANY)
STATE = [pltpu.VMEM((2 * ROWS, HALF), jnp.float32)] * 3
TOKEN = [pltpu.VMEM((8, 128), jnp.float32)]
POS, LOW_FIRST, LOW_LAST, MINE, SLOT = 1, 5, 9, 13, 17


def params(limit=VLIM):
    return pltpu.CompilerParams(vmem_limit_bytes=limit)


def cost(micros):
    return pl.CostEstimate(
        flops=int(micros * 1.15e9), bytes_accessed=1 << 20, transcendentals=1 << 20
    )


def fast(x):
    return pltpu.with_memory_space_constraint(x, pltpu.VMEM)


def touch(buffer, token):
    return pl.pallas_call(
        lambda buffer_ref, token_ref, out_ref: None,
        out_shape=pltpu.VMEM(buffer.shape, buffer.dtype),
        in_specs=[ASPEC, ASPEC],
        out_specs=ASPEC,
        input_output_aliases={0: 0},
        compiler_params=params(1024 * 1024),
        name="touch",
    )(fast(buffer), fast(token))


def span(index, width):
    return pl.ds(pl.multiple_of(index * width, width), width)


def run_copies(moves, sems):
    copies = [
        pltpu.make_async_copy(source, target, sems.at[i])
        for i, (source, target) in enumerate(moves)
    ]
    for copy in copies:
        copy.start()
    for copy in copies:
        copy.wait()


def near_kernel(k, v, near, cross, sems):
    core = lax.rem(lax.axis_index("seq"), 2)
    moves = []
    for target, half in ((near, core), (cross, 1 - core)):
        for i, source in enumerate((k, v)):
            moves.append((source.at[:, span(half, 256)], target.at[:, i * 256 : i * 256 + 256]))
    run_copies(moves, sems)


def pack_kernel(q, cross, lengths, home, swap, own, lengths_here, home_here, sems):
    core = lax.rem(lax.axis_index("seq"), 2)
    moves = [
        (q.at[:, span(1 - core, HALF)], swap.at[:, 0:HALF]),
        (q.at[:, span(core, HALF)], own),
        (cross, swap.at[:, HALF : HALF + KVW]),
        (lengths, lengths_here),
        (home, home_here),
    ]
    run_copies(moves, sems)


def plan_kernel(lengths, home, meta, low_key):
    device = lax.axis_index("seq")
    core = lax.rem(device, 2)
    docs = lengths.shape[1]
    wide = jnp.broadcast_to(lengths[...].astype(jnp.float32), (docs, docs))
    before = lax.broadcasted_iota(jnp.int32, (docs, docs), 0) < lax.broadcasted_iota(
        jnp.int32, (docs, docs), 1
    )
    starts = jnp.sum(jnp.where(before, wide.T, jnp.float32(0.0)), axis=0, keepdims=True)
    meta[0] = core
    for block in range(4):
        half = device if block < 2 else device + 1 - 2 * core
        pos = half * ROWS + (block % 2) * BLOCK
        meta[POS + block] = pos
        for slot, shift in ((LOW_FIRST, 0), (LOW_LAST, BLOCK - 1)):
            at = (pos + shift).astype(jnp.float32)
            first = jnp.max(jnp.where(starts <= at, starts, jnp.float32(0.0)))
            meta[slot + block] = jnp.maximum(
                first.astype(jnp.int32), pos + shift - (WINDOW - 1)
            )
        rows = (pos + lax.broadcasted_iota(jnp.int32, (BLOCK, docs), 0)).astype(jnp.float32)
        first = jnp.max(
            jnp.where(starts <= rows, starts, jnp.float32(0.0)), axis=1, keepdims=True
        )
        low_key[pl.ds(block * BLOCK, BLOCK), :] = jnp.maximum(
            jnp.broadcast_to(first, (BLOCK, docs)), rows - (WINDOW - 1)
        ).astype(jnp.int32)
    homes = [home[(device - core) * 2 + t] for t in range(4)]
    for t in range(4):
        rank = jnp.int32(0)
        for u in range(t):
            rank = rank + (homes[u] == homes[t]).astype(jnp.int32)
        place = lax.rem(t + 2 * core, 4)
        meta[MINE + place] = (homes[t] == device).astype(jnp.int32)
        meta[SLOT + place] = rank


def row_span(row):
    return pl.ds(row if isinstance(row, int) else pl.multiple_of(row, BLOCK), BLOCK)


def stacked(ref, rows, kvh):
    return jnp.concatenate(
        [ref[rows, pl.ds((kvh * GROUP + g) * HD, HD)] for g in range(GROUP)], axis=0
    )


def fold(q, kv, kv_row, state, row, bias=None, first=False, width=ROWS):
    acc, top, low = state
    rows = row_span(row)
    key_rows = pl.ds(kv_row, width)
    for kvh in range(HEADS // GROUP):
        keys = kv[key_rows, kvh * HD : (kvh + 1) * HD]
        vals = kv[key_rows, 256 + kvh * HD : 256 + (kvh + 1) * HD]
        scores = (
            lax.dot_general(
                stacked(q, rows, kvh),
                keys,
                (((1,), (1,)), ((), ())),
                preferred_element_type=jnp.float32,
            )
            * FACTOR
        )
        if bias is not None:
            scores = scores + jnp.concatenate([bias] * GROUP, axis=0)
        peak = jnp.max(scores, axis=1, keepdims=True)
        if first:
            new = jnp.broadcast_to(peak, (GROUP * BLOCK, HD))
        else:
            old = stacked(top, rows, kvh)
            new = jnp.maximum(old, peak)
            keep = jnp.exp2(old - new)
        weights = jnp.exp2(scores - jnp.concatenate([new] * (width // HD), axis=1))
        mixed = jnp.dot(weights.astype(jnp.bfloat16), vals, preferred_element_type=jnp.float32)
        part = weights[:, :HD]
        if width > HD:
            part = part + weights[:, HD:]
        for g in range(GROUP):
            cols = pl.ds((kvh * GROUP + g) * HD, HD)
            cut = slice(g * BLOCK, (g + 1) * BLOCK)
            top[rows, cols] = new[cut]
            if first:
                low[rows, cols] = part[cut]
                acc[rows, cols] = mixed[cut]
            else:
                low[rows, cols] = low[rows, cols] * keep[cut] + part[cut]
                acc[rows, cols] = acc[rows, cols] * keep[cut] + mixed[cut]


def bias_of(meta, low_key, block, key_base, span=ROWS):
    last = meta[POS + block] + lax.broadcasted_iota(jnp.int32, (BLOCK, HD), 0)
    least = low_key[row_span(block * BLOCK), :]
    parts = []
    for start in range(0, span, HD):
        key = key_base + start + lax.broadcasted_iota(jnp.int32, (BLOCK, HD), 1)
        allowed = (key <= last) & (key >= least)
        parts.append(jnp.where(allowed, jnp.float32(0.0), jnp.float32(NEG)))
    return jnp.concatenate(parts, axis=1)


def half_update(meta, low_key, q, kv, kv_row, half, key_base, state):
    block = half * 2
    last_key = key_base + ROWS - 1
    some = (key_base <= meta[POS + block + 1] + BLOCK - 1) & (last_key >= meta[LOW_FIRST + block])
    full = (last_key <= meta[POS + block]) & (key_base >= meta[LOW_LAST + block + 1])

    @pl.when(full)
    def _():
        for step in range(2):
            fold(q, kv, kv_row, state, (block + step) * BLOCK)

    @pl.when(some & jnp.logical_not(full))
    def _():
        for step in range(2):
            bias = bias_of(meta, low_key, block + step, key_base)
            fold(q, kv, kv_row, state, (block + step) * BLOCK, bias)


def first_kernel(meta, low_key, own, near, recv, q, acc, top, low, token, kv):
    state = (acc, top, low)
    q[0:ROWS, :] = own[...]
    q[ROWS : 2 * ROWS, :] = recv[:, 0:HALF]
    kv[0:ROWS, :] = near[...]
    kv[ROWS : 2 * ROWS, :] = recv[:, HALF : HALF + KVW]

    def body(half, carry):
        kv_row = pl.multiple_of(half * ROWS, ROWS)
        base = meta[POS + half * 2]
        for step in range(2):
            span = (step + 1) * BLOCK
            block = half * 2 + step
            bias = bias_of(meta, low_key, block, base, span)
            fold(q, kv, kv_row, state, block * BLOCK, bias, True, span)
        return carry

    lax.fori_loop(0, 2, body, 0)
    late = 1 - meta[0]
    early_row = pl.multiple_of((1 - late) * ROWS, ROWS)
    half_update(meta, low_key, q, kv, early_row, late, meta[POS + 2 - late * 2], state)


def next_kernel(back, side, meta, low_key, q, kv, *refs):
    state = refs[3:6]
    base = meta[POS + side * 2] - back * 2 * ROWS

    def body(half, carry):
        half_update(meta, low_key, q, kv, 0, half, base, state)
        return carry

    lax.fori_loop(0, 2, body, 0)


def last_kernel(back, side, meta, low_key, q, kv, a, t, d, keep, send, acc, top, low):
    next_kernel(back, side, meta, low_key, q, kv, a, t, d, acc, top, low)

    def body(block, carry):
        rows = row_span(block * BLOCK)
        slot = pl.ds(pl.multiple_of(meta[SLOT + block] * BLOCK, BLOCK), BLOCK)

        def write(ref, rows=rows, slot=slot):
            for head in range(HEADS):
                cols = pl.ds(head * HD, HD)
                total = jnp.sum(low[rows, cols], axis=1, keepdims=True)
                ref[slot, cols] = (acc[rows, cols] * (1.0 / total)).astype(jnp.bfloat16)

        @pl.when(meta[MINE + block] == 1)
        def _(write=write):
            write(keep)

        @pl.when(meta[MINE + block] == 0)
        def _(write=write):
            write(send)

        return carry

    lax.fori_loop(0, 4, body, 0)


def join_kernel(keep, got, out, sems):
    core = lax.rem(lax.axis_index("seq"), 2)
    run_copies(
        [(keep, out.at[:, span(core, HALF)]), (got, out.at[:, span(1 - core, HALF)])], sems
    )


def local(queries, keys, values, lengths, home):
    count = lax.axis_size("seq")
    bf16 = jnp.bfloat16
    hbm = pl.BlockSpec(memory_space=pltpu.HBM)
    near, cross = pl.pallas_call(
        near_kernel,
        out_shape=[pltpu.VMEM((ROWS, KVW), bf16)] * 2,
        in_specs=[hbm] * 2,
        out_specs=[VSPEC] * 2,
        scratch_shapes=[pltpu.SemaphoreType.DMA((4,))],
        compiler_params=params(60 * 1024 * 1024),
        name="near",
    )(keys, values)
    lengths = lengths[None, :]
    swap, own, lengths, home = pl.pallas_call(
        pack_kernel,
        out_shape=[
            pltpu.VMEM((ROWS, HALF + KVW), bf16),
            pltpu.VMEM((ROWS, HALF), bf16),
            pltpu.VMEM(lengths.shape, jnp.int32),
            pltpu.SMEM(home.shape, jnp.int32),
        ],
        in_specs=[hbm, VSPEC, hbm, hbm],
        out_specs=[VSPEC] * 3 + [SSPEC],
        scratch_shapes=[pltpu.SemaphoreType.DMA((5,))],
        compiler_params=params(60 * 1024 * 1024),
        name="pack",
    )(queries, fast(cross), lengths, home)

    same = [(i, i + 2) for i in range(count - 2)]
    other = [(i, (i ^ 1) + 2) for i in range(count - 2)]
    pair = [(i, i ^ 1) for i in range(count)]
    shift = functools.partial(lax.ppermute, axis_name="seq")
    arrived = [shift(cross, perm=other), shift(near, perm=same)]
    recv = fast(shift(swap, perm=pair))

    meta, low_key = pl.pallas_call(
        plan_kernel,
        out_shape=[pltpu.SMEM((32,), jnp.int32), pltpu.VMEM((2 * ROWS, HD), jnp.int32)],
        in_specs=[VSPEC, SSPEC],
        out_specs=[SSPEC, VSPEC],
        compiler_params=params(),
        cost_estimate=cost(PLAN),
        name="plan",
    )(fast(lengths), pltpu.with_memory_space_constraint(home, pltpu.SMEM))
    meta = pltpu.with_memory_space_constraint(meta, pltpu.SMEM)
    low_key, own = fast(low_key), fast(own)

    q, *state, token = pl.pallas_call(
        first_kernel,
        out_shape=[pltpu.VMEM((2 * ROWS, HALF), bf16)] + STATE + TOKEN,
        in_specs=[SSPEC] + [VSPEC] * 4,
        out_specs=[VSPEC] * 4 + [ASPEC],
        scratch_shapes=[pltpu.VMEM((2 * ROWS, KVW), bf16)],
        compiler_params=params(),
        cost_estimate=cost(3.0),
        name="first",
    )(meta, low_key, own, fast(near), recv)
    tokens = [None, token]
    for index in range(6):
        kv = arrived[index]
        if index:
            kv = arrived[index] = touch(kv, tokens[index])
        arrived.append(shift(kv, perm=same))
        if index == 0:
            continue
        state, token = step(index - 1, arrived, meta, low_key, q, state)
        tokens.append(token)
    for index in (5, 6):
        state, token = step(index, arrived, meta, low_key, q, state)
    keep, send = step(7, arrived, meta, low_key, q, state)
    got = shift(send, perm=pair)
    return pl.pallas_call(
        join_kernel,
        out_shape=jax.ShapeDtypeStruct((ROWS, 2 * HALF), bf16),
        in_specs=[VSPEC] * 2,
        out_specs=pl.BlockSpec(memory_space=pltpu.HBM),
        scratch_shapes=[pltpu.SemaphoreType.DMA((2,))],
        compiler_params=params(),
        name="join",
    )(fast(keep), fast(got))


def step(index, arrived, meta, low_key, q, state):
    last = index == 7
    kernel = last_kernel if last else next_kernel
    extra = [pltpu.VMEM((ROWS, HALF), jnp.bfloat16)] * 2 if last else []
    results = pl.pallas_call(
        functools.partial(kernel, index // 2 + 1, 1 - index % 2),
        out_shape=extra + STATE + ([] if last else TOKEN),
        in_specs=[SSPEC] + [VSPEC] * 6,
        out_specs=[VSPEC] * (len(extra) + 3) + ([] if last else [ASPEC]),
        input_output_aliases={4 + i: len(extra) + i for i in range(3)},
        compiler_params=params(),
        cost_estimate=cost(1.0),
        name="last" if last else "next",
    )(meta, low_key, fast(q), fast(arrived[index]), *[fast(x) for x in state])
    return results[:2] if last else (results[:3], results[3])


def solution(mesh):
    placed = (
        P(("pack", "seq"), None),
        P(("pack", "seq"), None),
        P(("pack", "seq"), None),
        P("pack"),
        P("pack"),
    )
    return jax.shard_map(
        local, mesh=mesh, in_specs=placed, out_specs=P(("pack", "seq"), None), check_vma=False
    )
```

```python
import functools
import math

import jax
import jax.numpy as jnp
from jax import lax
from jax.experimental import pallas as pl
from jax.experimental.pallas import tpu as pltpu
from jax.sharding import PartitionSpec as P

HD = 128
BLOCK = 128
WINDOW = 2048
ROWS = 256
HEADS = 8
GROUP = 4
HALF = HEADS * HD
KVW = 512
FACTOR = HD**-0.5 * math.log2(math.e)
NEG = -1e30
PLAN = 20.0
VLIM = 24 * 1024 * 1024
VSPEC = pl.BlockSpec(memory_space=pltpu.VMEM)
SSPEC = pl.BlockSpec(memory_space=pltpu.SMEM)
ASPEC = pl.BlockSpec(memory_space=pl.ANY)
STATE = [pltpu.VMEM((2 * ROWS, HALF), jnp.float32)] * 3
TOKEN = [pltpu.VMEM((8, 128), jnp.float32)]
POS, LOW_FIRST, LOW_LAST, MINE, SLOT = 1, 5, 9, 13, 17


def params(limit=VLIM):
    return pltpu.CompilerParams(vmem_limit_bytes=limit)


def cost(micros):
    return pl.CostEstimate(
        flops=int(micros * 1.15e9), bytes_accessed=1 << 20, transcendentals=1 << 20
    )


def fast(x):
    return pltpu.with_memory_space_constraint(x, pltpu.VMEM)


def touch(buffer, token):
    return pl.pallas_call(
        lambda buffer_ref, token_ref, out_ref: None,
        out_shape=pltpu.VMEM(buffer.shape, buffer.dtype),
        in_specs=[ASPEC, ASPEC],
        out_specs=ASPEC,
        input_output_aliases={0: 0},
        compiler_params=params(1024 * 1024),
        name="touch",
    )(fast(buffer), fast(token))


def span(index, width):
    return pl.ds(pl.multiple_of(index * width, width), width)


def run_copies(moves, sems):
    copies = [
        pltpu.make_async_copy(source, target, sems.at[i])
        for i, (source, target) in enumerate(moves)
    ]
    for copy in copies:
        copy.start()
    for copy in copies:
        copy.wait()


def near_kernel(k, v, near, cross, sems):
    core = lax.rem(lax.axis_index("seq"), 2)
    moves = []
    for target, half in ((near, core), (cross, 1 - core)):
        for i, source in enumerate((k, v)):
            moves.append((source.at[:, span(half, 256)], target.at[:, i * 256 : i * 256 + 256]))
    run_copies(moves, sems)


def pack_kernel(q, cross, lengths, home, swap, own, lengths_here, home_here, sems):
    core = lax.rem(lax.axis_index("seq"), 2)
    moves = [
        (q.at[:, span(1 - core, HALF)], swap.at[:, 0:HALF]),
        (q.at[:, span(core, HALF)], own),
        (cross, swap.at[:, HALF : HALF + KVW]),
        (lengths, lengths_here),
        (home, home_here),
    ]
    run_copies(moves, sems)


def plan_kernel(lengths, home, meta, low_key):
    device = lax.axis_index("seq")
    core = lax.rem(device, 2)
    docs = lengths.shape[1]
    wide = jnp.broadcast_to(lengths[...].astype(jnp.float32), (docs, docs))
    before = lax.broadcasted_iota(jnp.int32, (docs, docs), 0) < lax.broadcasted_iota(
        jnp.int32, (docs, docs), 1
    )
    starts = jnp.sum(jnp.where(before, wide.T, jnp.float32(0.0)), axis=0, keepdims=True)
    meta[0] = core
    for block in range(4):
        half = device if block < 2 else device + 1 - 2 * core
        pos = half * ROWS + (block % 2) * BLOCK
        meta[POS + block] = pos
        for slot, shift in ((LOW_FIRST, 0), (LOW_LAST, BLOCK - 1)):
            at = (pos + shift).astype(jnp.float32)
            first = jnp.max(jnp.where(starts <= at, starts, jnp.float32(0.0)))
            meta[slot + block] = jnp.maximum(
                first.astype(jnp.int32), pos + shift - (WINDOW - 1)
            )
        rows = (pos + lax.broadcasted_iota(jnp.int32, (BLOCK, docs), 0)).astype(jnp.float32)
        first = jnp.max(
            jnp.where(starts <= rows, starts, jnp.float32(0.0)), axis=1, keepdims=True
        )
        low_key[pl.ds(block * BLOCK, BLOCK), :] = jnp.maximum(
            jnp.broadcast_to(first, (BLOCK, docs)), rows - (WINDOW - 1)
        ).astype(jnp.int32)
    homes = [home[(device - core) * 2 + t] for t in range(4)]
    for t in range(4):
        rank = jnp.int32(0)
        for u in range(t):
            rank = rank + (homes[u] == homes[t]).astype(jnp.int32)
        place = lax.rem(t + 2 * core, 4)
        meta[MINE + place] = (homes[t] == device).astype(jnp.int32)
        meta[SLOT + place] = rank


def row_span(row):
    return pl.ds(row if isinstance(row, int) else pl.multiple_of(row, BLOCK), BLOCK)


def stacked(ref, rows, kvh):
    return jnp.concatenate(
        [ref[rows, pl.ds((kvh * GROUP + g) * HD, HD)] for g in range(GROUP)], axis=0
    )


def fold(q, kv, kv_row, state, row, bias=None, first=False, width=ROWS):
    acc, top, low = state
    rows = row_span(row)
    key_rows = pl.ds(kv_row, width)
    for kvh in range(HEADS // GROUP):
        keys = kv[key_rows, kvh * HD : (kvh + 1) * HD]
        vals = kv[key_rows, 256 + kvh * HD : 256 + (kvh + 1) * HD]
        scores = (
            lax.dot_general(
                stacked(q, rows, kvh),
                keys,
                (((1,), (1,)), ((), ())),
                preferred_element_type=jnp.float32,
            )
            * FACTOR
        )
        if bias is not None:
            scores = scores + jnp.concatenate([bias] * GROUP, axis=0)
        peak = jnp.max(scores, axis=1, keepdims=True)
        if first:
            new = jnp.broadcast_to(peak, (GROUP * BLOCK, HD))
        else:
            old = stacked(top, rows, kvh)
            new = jnp.maximum(old, peak)
            keep = jnp.exp2(old - new)
        weights = jnp.exp2(scores - jnp.concatenate([new] * (width // HD), axis=1))
        mixed = jnp.dot(weights.astype(jnp.bfloat16), vals, preferred_element_type=jnp.float32)
        part = weights[:, :HD]
        if width > HD:
            part = part + weights[:, HD:]
        for g in range(GROUP):
            cols = pl.ds((kvh * GROUP + g) * HD, HD)
            cut = slice(g * BLOCK, (g + 1) * BLOCK)
            top[rows, cols] = new[cut]
            if first:
                low[rows, cols] = part[cut]
                acc[rows, cols] = mixed[cut]
            else:
                low[rows, cols] = low[rows, cols] * keep[cut] + part[cut]
                acc[rows, cols] = acc[rows, cols] * keep[cut] + mixed[cut]


def bias_of(meta, low_key, block, key_base, span=ROWS):
    last = meta[POS + block] + lax.broadcasted_iota(jnp.int32, (BLOCK, HD), 0)
    least = low_key[row_span(block * BLOCK), :]
    parts = []
    for start in range(0, span, HD):
        key = key_base + start + lax.broadcasted_iota(jnp.int32, (BLOCK, HD), 1)
        allowed = (key <= last) & (key >= least)
        parts.append(jnp.where(allowed, jnp.float32(0.0), jnp.float32(NEG)))
    return jnp.concatenate(parts, axis=1)


def half_update(meta, low_key, q, kv, kv_row, half, key_base, state):
    block = half * 2
    last_key = key_base + ROWS - 1
    some = (key_base <= meta[POS + block + 1] + BLOCK - 1) & (last_key >= meta[LOW_FIRST + block])
    full = (last_key <= meta[POS + block]) & (key_base >= meta[LOW_LAST + block + 1])

    @pl.when(full)
    def _():
        for step in range(2):
            fold(q, kv, kv_row, state, (block + step) * BLOCK)

    @pl.when(some & jnp.logical_not(full))
    def _():
        for step in range(2):
            bias = bias_of(meta, low_key, block + step, key_base)
            fold(q, kv, kv_row, state, (block + step) * BLOCK, bias)


def first_kernel(meta, low_key, own, near, recv, q, acc, top, low, token, kv):
    state = (acc, top, low)
    q[0:ROWS, :] = own[...]
    q[ROWS : 2 * ROWS, :] = recv[:, 0:HALF]
    kv[0:ROWS, :] = near[...]
    kv[ROWS : 2 * ROWS, :] = recv[:, HALF : HALF + KVW]

    def body(half, carry):
        kv_row = pl.multiple_of(half * ROWS, ROWS)
        base = meta[POS + half * 2]
        for step in range(2):
            span = (step + 1) * BLOCK
            block = half * 2 + step
            bias = bias_of(meta, low_key, block, base, span)
            fold(q, kv, kv_row, state, block * BLOCK, bias, True, span)
        return carry

    lax.fori_loop(0, 2, body, 0)
    late = 1 - meta[0]
    early_row = pl.multiple_of((1 - late) * ROWS, ROWS)
    half_update(meta, low_key, q, kv, early_row, late, meta[POS + 2 - late * 2], state)


def next_kernel(back, side, meta, low_key, q, kv, *refs):
    state = refs[3:6]
    base = meta[POS + side * 2] - back * 2 * ROWS

    def body(half, carry):
        half_update(meta, low_key, q, kv, 0, half, base, state)
        return carry

    lax.fori_loop(0, 2, body, 0)


def write_blocks(meta, acc, low, target, mine):
    def body(block, carry):
        rows = row_span(block * BLOCK)
        slot = row_span(meta[SLOT + block] * BLOCK)

        @pl.when(meta[MINE + block] == mine)
        def _():
            for head in range(HEADS):
                cols = pl.ds(head * HD, HD)
                total = jnp.sum(low[rows, cols], axis=1, keepdims=True)
                target[slot, cols] = (acc[rows, cols] * (1.0 / total)).astype(jnp.bfloat16)

        return carry

    lax.fori_loop(0, 4, body, 0)


def last_kernel(back, side, meta, low_key, q, kv, a, t, d, send, acc, top, low):
    next_kernel(back, side, meta, low_key, q, kv, a, t, d, acc, top, low)
    write_blocks(meta, acc, low, send, 0)


def keep_kernel(meta, acc, low, out, kept, sems):
    write_blocks(meta, acc, low, kept, 1)
    run_copies([(kept, out.at[:, span(meta[0], HALF)])], sems)


def join_kernel(got, partial, out, sems):
    core = lax.rem(lax.axis_index("seq"), 2)
    run_copies([(got, out.at[:, span(1 - core, HALF)])], sems)


def local(queries, keys, values, lengths, home):
    count = lax.axis_size("seq")
    bf16 = jnp.bfloat16
    hbm = pl.BlockSpec(memory_space=pltpu.HBM)
    near, cross = pl.pallas_call(
        near_kernel,
        out_shape=[pltpu.VMEM((ROWS, KVW), bf16)] * 2,
        in_specs=[hbm] * 2,
        out_specs=[VSPEC] * 2,
        scratch_shapes=[pltpu.SemaphoreType.DMA((4,))],
        compiler_params=params(60 * 1024 * 1024),
        name="near",
    )(keys, values)
    lengths = lengths[None, :]
    swap, own, lengths, home = pl.pallas_call(
        pack_kernel,
        out_shape=[
            pltpu.VMEM((ROWS, HALF + KVW), bf16),
            pltpu.VMEM((ROWS, HALF), bf16),
            pltpu.VMEM(lengths.shape, jnp.int32),
            pltpu.SMEM(home.shape, jnp.int32),
        ],
        in_specs=[hbm, VSPEC, hbm, hbm],
        out_specs=[VSPEC] * 3 + [SSPEC],
        scratch_shapes=[pltpu.SemaphoreType.DMA((5,))],
        compiler_params=params(60 * 1024 * 1024),
        name="pack",
    )(queries, fast(cross), lengths, home)

    same = [(i, i + 2) for i in range(count - 2)]
    other = [(i, (i ^ 1) + 2) for i in range(count - 2)]
    pair = [(i, i ^ 1) for i in range(count)]
    shift = functools.partial(lax.ppermute, axis_name="seq")
    arrived = [shift(cross, perm=other), shift(near, perm=same)]
    recv = fast(shift(swap, perm=pair))

    meta, low_key = pl.pallas_call(
        plan_kernel,
        out_shape=[pltpu.SMEM((32,), jnp.int32), pltpu.VMEM((2 * ROWS, HD), jnp.int32)],
        in_specs=[VSPEC, SSPEC],
        out_specs=[SSPEC, VSPEC],
        compiler_params=params(),
        cost_estimate=cost(PLAN),
        name="plan",
    )(fast(lengths), pltpu.with_memory_space_constraint(home, pltpu.SMEM))
    meta = pltpu.with_memory_space_constraint(meta, pltpu.SMEM)
    low_key, own = fast(low_key), fast(own)

    q, *state, token = pl.pallas_call(
        first_kernel,
        out_shape=[pltpu.VMEM((2 * ROWS, HALF), bf16)] + STATE + TOKEN,
        in_specs=[SSPEC] + [VSPEC] * 4,
        out_specs=[VSPEC] * 4 + [ASPEC],
        scratch_shapes=[pltpu.VMEM((2 * ROWS, KVW), bf16)],
        compiler_params=params(),
        cost_estimate=cost(3.0),
        name="first",
    )(meta, low_key, own, fast(near), recv)
    tokens = [None, token]
    for index in range(6):
        kv = arrived[index]
        if index:
            kv = arrived[index] = touch(kv, tokens[index])
        arrived.append(shift(kv, perm=same))
        if index == 0:
            continue
        state, token = step(index - 1, arrived, meta, low_key, q, state)
        tokens.append(token)
    for index in (5, 6):
        state, token = step(index, arrived, meta, low_key, q, state)
    send, acc, low = step(7, arrived, meta, low_key, q, state)
    got = shift(send, perm=pair)
    partial = pl.pallas_call(
        keep_kernel,
        out_shape=pltpu.HBM((ROWS, 2 * HALF), bf16),
        in_specs=[SSPEC, VSPEC, VSPEC],
        out_specs=hbm,
        scratch_shapes=[pltpu.VMEM((ROWS, HALF), bf16), pltpu.SemaphoreType.DMA((1,))],
        compiler_params=params(),
        cost_estimate=cost(0.5),
        name="keep",
    )(meta, fast(acc), fast(low))
    return pl.pallas_call(
        join_kernel,
        out_shape=jax.ShapeDtypeStruct((ROWS, 2 * HALF), bf16),
        in_specs=[VSPEC, hbm],
        out_specs=hbm,
        input_output_aliases={1: 0},
        scratch_shapes=[pltpu.SemaphoreType.DMA((1,))],
        compiler_params=params(),
        name="join",
    )(fast(got), partial)


def step(index, arrived, meta, low_key, q, state):
    last = index == 7
    kernel = last_kernel if last else next_kernel
    extra = [pltpu.VMEM((ROWS, HALF), jnp.bfloat16)] if last else []
    results = pl.pallas_call(
        functools.partial(kernel, index // 2 + 1, 1 - index % 2),
        out_shape=extra + STATE + ([] if last else TOKEN),
        in_specs=[SSPEC] + [VSPEC] * 6,
        out_specs=[VSPEC] * (len(extra) + 3) + ([] if last else [ASPEC]),
        input_output_aliases={4 + i: len(extra) + i for i in range(3)},
        compiler_params=params(),
        cost_estimate=cost(1.0),
        name="last" if last else "next",
    )(meta, low_key, fast(q), fast(arrived[index]), *[fast(x) for x in state])
    return (results[0], results[1], results[3]) if last else (results[:3], results[3])


def solution(mesh):
    placed = (
        P(("pack", "seq"), None),
        P(("pack", "seq"), None),
        P(("pack", "seq"), None),
        P("pack"),
        P("pack"),
    )
    return jax.shard_map(
        local, mesh=mesh, in_specs=placed, out_specs=P(("pack", "seq"), None), check_vma=False
    )
```

```python
import functools
import math

import jax
import jax.numpy as jnp
from jax import lax
from jax.experimental import pallas as pl
from jax.experimental.pallas import tpu as pltpu
from jax.sharding import PartitionSpec as P

HD = 128
BLOCK = 128
WINDOW = 2048
ROWS = 256
HEADS = 8
GROUP = 4
HALF = HEADS * HD
KVW = 512
FACTOR = HD**-0.5 * math.log2(math.e)
NEG = -1e30
PLAN = 20.0
VLIM = 24 * 1024 * 1024
VSPEC = pl.BlockSpec(memory_space=pltpu.VMEM)
SSPEC = pl.BlockSpec(memory_space=pltpu.SMEM)
ASPEC = pl.BlockSpec(memory_space=pl.ANY)
STATE = [pltpu.VMEM((2 * ROWS, HALF), jnp.float32)] * 3
TOKEN = [pltpu.VMEM((8, 128), jnp.float32)]
POS, LOW_FIRST, LOW_LAST, MINE, SLOT = 1, 5, 9, 13, 17


def params(limit=VLIM):
    return pltpu.CompilerParams(vmem_limit_bytes=limit)


def cost(micros):
    return pl.CostEstimate(
        flops=int(micros * 1.15e9), bytes_accessed=1 << 20, transcendentals=1 << 20
    )


def fast(x):
    return pltpu.with_memory_space_constraint(x, pltpu.VMEM)


def touch(buffer, token):
    return pl.pallas_call(
        lambda buffer_ref, token_ref, out_ref: None,
        out_shape=pltpu.VMEM(buffer.shape, buffer.dtype),
        in_specs=[ASPEC, ASPEC],
        out_specs=ASPEC,
        input_output_aliases={0: 0},
        compiler_params=params(1024 * 1024),
        name="touch",
    )(fast(buffer), fast(token))


def span(index, width):
    return pl.ds(pl.multiple_of(index * width, width), width)


def run_copies(moves, sems):
    copies = [
        pltpu.make_async_copy(source, target, sems.at[i])
        for i, (source, target) in enumerate(moves)
    ]
    for copy in copies:
        copy.start()
    for copy in copies:
        copy.wait()


def near_kernel(k, v, near, cross, sems):
    core = lax.rem(lax.axis_index("seq"), 2)
    moves = []
    for target, half in ((near, core), (cross, 1 - core)):
        for i, source in enumerate((k, v)):
            moves.append((source.at[:, span(half, 256)], target.at[:, i * 256 : i * 256 + 256]))
    run_copies(moves, sems)


def pack_kernel(q, cross, lengths, home, swap, own, lengths_here, home_here, sems):
    core = lax.rem(lax.axis_index("seq"), 2)
    moves = [
        (q.at[:, span(1 - core, HALF)], swap.at[:, 0:HALF]),
        (q.at[:, span(core, HALF)], own),
        (cross, swap.at[:, HALF : HALF + KVW]),
        (lengths, lengths_here),
        (home, home_here),
    ]
    run_copies(moves, sems)


def plan_kernel(lengths, home, meta, low_key):
    device = lax.axis_index("seq")
    core = lax.rem(device, 2)
    docs = lengths.shape[1]
    wide = jnp.broadcast_to(lengths[...].astype(jnp.float32), (docs, docs))
    before = lax.broadcasted_iota(jnp.int32, (docs, docs), 0) < lax.broadcasted_iota(
        jnp.int32, (docs, docs), 1
    )
    starts = jnp.sum(jnp.where(before, wide.T, jnp.float32(0.0)), axis=0, keepdims=True)
    meta[0] = core
    for block in range(4):
        half = device if block < 2 else device + 1 - 2 * core
        pos = half * ROWS + (block % 2) * BLOCK
        meta[POS + block] = pos
        for slot, shift in ((LOW_FIRST, 0), (LOW_LAST, BLOCK - 1)):
            at = (pos + shift).astype(jnp.float32)
            first = jnp.max(jnp.where(starts <= at, starts, jnp.float32(0.0)))
            meta[slot + block] = jnp.maximum(
                first.astype(jnp.int32), pos + shift - (WINDOW - 1)
            )
        rows = (pos + lax.broadcasted_iota(jnp.int32, (BLOCK, docs), 0)).astype(jnp.float32)
        first = jnp.max(
            jnp.where(starts <= rows, starts, jnp.float32(0.0)), axis=1, keepdims=True
        )
        low_key[pl.ds(block * BLOCK, BLOCK), :] = jnp.maximum(
            jnp.broadcast_to(first, (BLOCK, docs)), rows - (WINDOW - 1)
        ).astype(jnp.int32)
    homes = [home[(device - core) * 2 + t] for t in range(4)]
    for t in range(4):
        rank = jnp.int32(0)
        for u in range(t):
            rank = rank + (homes[u] == homes[t]).astype(jnp.int32)
        place = lax.rem(t + 2 * core, 4)
        meta[MINE + place] = (homes[t] == device).astype(jnp.int32)
        meta[SLOT + place] = rank


def row_span(row):
    return pl.ds(row if isinstance(row, int) else pl.multiple_of(row, BLOCK), BLOCK)


def stacked(ref, rows, kvh):
    return jnp.concatenate(
        [ref[rows, pl.ds((kvh * GROUP + g) * HD, HD)] for g in range(GROUP)], axis=0
    )


def fold(q, kv, kv_row, state, row, bias=None, first=False, width=ROWS):
    acc, top, low = state
    rows = row_span(row)
    key_rows = pl.ds(kv_row, width)
    for kvh in range(HEADS // GROUP):
        keys = kv[key_rows, kvh * HD : (kvh + 1) * HD]
        vals = kv[key_rows, 256 + kvh * HD : 256 + (kvh + 1) * HD]
        scores = (
            lax.dot_general(
                stacked(q, rows, kvh),
                keys,
                (((1,), (1,)), ((), ())),
                preferred_element_type=jnp.float32,
            )
            * FACTOR
        )
        if bias is not None:
            scores = scores + jnp.concatenate([bias] * GROUP, axis=0)
        peak = jnp.max(scores, axis=1, keepdims=True)
        if first:
            new = jnp.broadcast_to(peak, (GROUP * BLOCK, HD))
        else:
            old = stacked(top, rows, kvh)
            new = jnp.maximum(old, peak)
            keep = jnp.exp2(old - new)
        weights = jnp.exp2(scores - jnp.concatenate([new] * (width // HD), axis=1))
        mixed = jnp.dot(weights.astype(jnp.bfloat16), vals, preferred_element_type=jnp.float32)
        part = weights[:, :HD]
        if width > HD:
            part = part + weights[:, HD:]
        for g in range(GROUP):
            cols = pl.ds((kvh * GROUP + g) * HD, HD)
            cut = slice(g * BLOCK, (g + 1) * BLOCK)
            top[rows, cols] = new[cut]
            if first:
                low[rows, cols] = part[cut]
                acc[rows, cols] = mixed[cut]
            else:
                low[rows, cols] = low[rows, cols] * keep[cut] + part[cut]
                acc[rows, cols] = acc[rows, cols] * keep[cut] + mixed[cut]


def bias_of(meta, low_key, block, key_base, span=ROWS):
    last = meta[POS + block] + lax.broadcasted_iota(jnp.int32, (BLOCK, HD), 0)
    least = low_key[row_span(block * BLOCK), :]
    parts = []
    for start in range(0, span, HD):
        key = key_base + start + lax.broadcasted_iota(jnp.int32, (BLOCK, HD), 1)
        allowed = (key <= last) & (key >= least)
        parts.append(jnp.where(allowed, jnp.float32(0.0), jnp.float32(NEG)))
    return jnp.concatenate(parts, axis=1)


def half_update(meta, low_key, q, kv, kv_row, half, key_base, state):
    block = half * 2
    last_key = key_base + ROWS - 1
    some = (key_base <= meta[POS + block + 1] + BLOCK - 1) & (last_key >= meta[LOW_FIRST + block])
    full = (last_key <= meta[POS + block]) & (key_base >= meta[LOW_LAST + block + 1])

    @pl.when(full)
    def _():
        for step in range(2):
            fold(q, kv, kv_row, state, (block + step) * BLOCK)

    @pl.when(some & jnp.logical_not(full))
    def _():
        for step in range(2):
            bias = bias_of(meta, low_key, block + step, key_base)
            fold(q, kv, kv_row, state, (block + step) * BLOCK, bias)


def first_kernel(meta, low_key, own, near, recv, q, acc, top, low, token, kv):
    state = (acc, top, low)
    q[0:ROWS, :] = own[...]
    q[ROWS : 2 * ROWS, :] = recv[:, 0:HALF]
    kv[0:ROWS, :] = near[...]
    kv[ROWS : 2 * ROWS, :] = recv[:, HALF : HALF + KVW]

    def body(half, carry):
        kv_row = pl.multiple_of(half * ROWS, ROWS)
        base = meta[POS + half * 2]
        for step in range(2):
            span = (step + 1) * BLOCK
            block = half * 2 + step
            bias = bias_of(meta, low_key, block, base, span)
            fold(q, kv, kv_row, state, block * BLOCK, bias, True, span)
        return carry

    lax.fori_loop(0, 2, body, 0)
    late = 1 - meta[0]
    early_row = pl.multiple_of((1 - late) * ROWS, ROWS)
    half_update(meta, low_key, q, kv, early_row, late, meta[POS + 2 - late * 2], state)


def next_kernel(back, side, meta, low_key, q, kv, *refs):
    state = refs[3:6]
    base = meta[POS + side * 2] - back * 2 * ROWS

    def body(half, carry):
        half_update(meta, low_key, q, kv, 0, half, base, state)
        return carry

    lax.fori_loop(0, 2, body, 0)


def write_blocks(meta, acc, low, target, mine):
    def body(block, carry):
        rows = row_span(block * BLOCK)
        slot = row_span(meta[SLOT + block] * BLOCK)

        @pl.when(meta[MINE + block] == mine)
        def _():
            for head in range(HEADS):
                cols = pl.ds(head * HD, HD)
                total = jnp.sum(low[rows, cols], axis=1, keepdims=True)
                target[slot, cols] = (acc[rows, cols] * (1.0 / total)).astype(jnp.bfloat16)

        return carry

    lax.fori_loop(0, 4, body, 0)


def last_kernel(back, side, meta, low_key, q, kv, a, t, d, send, acc, top, low):
    next_kernel(back, side, meta, low_key, q, kv, a, t, d, acc, top, low)
    write_blocks(meta, acc, low, send, 0)


def keep_kernel(meta, acc, low, out, kept, sems):
    write_blocks(meta, acc, low, kept, 1)
    run_copies([(kept, out.at[:, span(meta[0], HALF)])], sems)


def join_kernel(got, partial, out, sems):
    core = lax.rem(lax.axis_index("seq"), 2)
    run_copies([(got, out.at[:, span(1 - core, HALF)])], sems)


def local(queries, keys, values, lengths, home):
    count = lax.axis_size("seq")
    bf16 = jnp.bfloat16
    hbm = pl.BlockSpec(memory_space=pltpu.HBM)
    near, cross = pl.pallas_call(
        near_kernel,
        out_shape=[pltpu.VMEM((ROWS, KVW), bf16)] * 2,
        in_specs=[hbm] * 2,
        out_specs=[VSPEC] * 2,
        scratch_shapes=[pltpu.SemaphoreType.DMA((4,))],
        compiler_params=params(60 * 1024 * 1024),
        name="near",
    )(keys, values)
    lengths = lengths[None, :]
    swap, own, lengths, home = pl.pallas_call(
        pack_kernel,
        out_shape=[
            pltpu.VMEM((ROWS, HALF + KVW), bf16),
            pltpu.VMEM((ROWS, HALF), bf16),
            pltpu.VMEM(lengths.shape, jnp.int32),
            pltpu.SMEM(home.shape, jnp.int32),
        ],
        in_specs=[hbm, VSPEC, hbm, hbm],
        out_specs=[VSPEC] * 3 + [SSPEC],
        scratch_shapes=[pltpu.SemaphoreType.DMA((5,))],
        compiler_params=params(60 * 1024 * 1024),
        name="pack",
    )(queries, fast(cross), lengths, home)

    same = [(i, i + 2) for i in range(count - 2)]
    other = [(i, (i ^ 1) + 2) for i in range(count - 2)]
    pair = [(i, i ^ 1) for i in range(count)]
    shift = functools.partial(lax.ppermute, axis_name="seq")
    arrived = [shift(cross, perm=other), shift(near, perm=same)]
    recv = fast(shift(swap, perm=pair))

    meta, low_key = pl.pallas_call(
        plan_kernel,
        out_shape=[pltpu.SMEM((32,), jnp.int32), pltpu.VMEM((2 * ROWS, HD), jnp.int32)],
        in_specs=[VSPEC, SSPEC],
        out_specs=[SSPEC, VSPEC],
        compiler_params=params(),
        cost_estimate=cost(PLAN),
        name="plan",
    )(fast(lengths), pltpu.with_memory_space_constraint(home, pltpu.SMEM))
    meta = pltpu.with_memory_space_constraint(meta, pltpu.SMEM)
    low_key, own = fast(low_key), fast(own)

    q, *state, token = pl.pallas_call(
        first_kernel,
        out_shape=[pltpu.VMEM((2 * ROWS, HALF), bf16)] + STATE + TOKEN,
        in_specs=[SSPEC] + [VSPEC] * 4,
        out_specs=[VSPEC] * 4 + [ASPEC],
        scratch_shapes=[pltpu.VMEM((2 * ROWS, KVW), bf16)],
        compiler_params=params(),
        cost_estimate=cost(3.0),
        name="first",
    )(meta, low_key, own, fast(near), recv)
    tokens = [None, token]
    for index in range(6):
        kv = arrived[index]
        if index > 1:
            kv = arrived[index] = touch(kv, tokens[index])
        arrived.append(shift(kv, perm=same))
        if index == 0:
            continue
        state, token = step(index - 1, arrived, meta, low_key, q, state)
        tokens.append(token)
    for index in (5, 6):
        state, token = step(index, arrived, meta, low_key, q, state)
    send, acc, low = step(7, arrived, meta, low_key, q, state)
    got = shift(send, perm=pair)
    partial = pl.pallas_call(
        keep_kernel,
        out_shape=pltpu.HBM((ROWS, 2 * HALF), bf16),
        in_specs=[SSPEC, VSPEC, VSPEC],
        out_specs=hbm,
        scratch_shapes=[pltpu.VMEM((ROWS, HALF), bf16), pltpu.SemaphoreType.DMA((1,))],
        compiler_params=params(),
        cost_estimate=cost(0.5),
        name="keep",
    )(meta, fast(acc), fast(low))
    return pl.pallas_call(
        join_kernel,
        out_shape=jax.ShapeDtypeStruct((ROWS, 2 * HALF), bf16),
        in_specs=[VSPEC, hbm],
        out_specs=hbm,
        input_output_aliases={1: 0},
        scratch_shapes=[pltpu.SemaphoreType.DMA((1,))],
        compiler_params=params(),
        name="join",
    )(fast(got), partial)


def step(index, arrived, meta, low_key, q, state):
    last = index == 7
    kernel = last_kernel if last else next_kernel
    extra = [pltpu.VMEM((ROWS, HALF), jnp.bfloat16)] if last else []
    results = pl.pallas_call(
        functools.partial(kernel, index // 2 + 1, 1 - index % 2),
        out_shape=extra + STATE + ([] if last else TOKEN),
        in_specs=[SSPEC] + [VSPEC] * 6,
        out_specs=[VSPEC] * (len(extra) + 3) + ([] if last else [ASPEC]),
        input_output_aliases={4 + i: len(extra) + i for i in range(3)},
        compiler_params=params(),
        cost_estimate=cost(1.0),
        name="last" if last else "next",
    )(meta, low_key, fast(q), fast(arrived[index]), *[fast(x) for x in state])
    return (results[0], results[1], results[3]) if last else (results[:3], results[3])


def solution(mesh):
    placed = (
        P(("pack", "seq"), None),
        P(("pack", "seq"), None),
        P(("pack", "seq"), None),
        P("pack"),
        P("pack"),
    )
    return jax.shard_map(
        local, mesh=mesh, in_specs=placed, out_specs=P(("pack", "seq"), None), check_vma=False
    )
```
